512 devices in a mesh: samp: 32 (over z, core), state: 16 (over x, y).
Axes of the slice: x: 4, y: 4, z: 16, core: 2. Of those that a mesh axis runs over, the one named last changes fastest.
Arguments:
- energies: float32 [16384, 64, 256], P(('samp', 'state')), may hold values from -170 to 90, as said below
- tile_rows: int32 [16384], P(('samp', 'state')), may hold values from 0 to 63, as said below
- tile_cols: int32 [16384], P(('samp', 'state')), may hold values from 0 to 16, as said below
- start_free: float32 [16384], P('state'), may hold values from -8 to 8
- temps: int32 [16384], P('state'), may hold values from 0 to 15
- betas: float32 [16], replicated, may hold values from 0.4 to 2.5
- counts: int32 [16384], P('state'), may hold values from 256 to 768
- basis: bfloat16 [32, 524288], P(None, 'samp'), may hold values from -6 to 6
Outputs:
- averages: float32 [32, 16384], P(None, 'state')
The draws below stay inside these ranges and needn't reach their ends.
Inputs may be any that keep to these rules, and one draw needn't show every extreme that they name: `tile_cols`: empty slots hold 16. On each device the live slots come first, their (row, column) pairs are distinct, and the live count lies between 1 and 32; in every column of devices along samp one device has all 32 slots live and covers each of its 16 state blocks. `tile_rows`: 0 on empty slots. `energies`: values of empty slots are arbitrary.
All inputs are finite; a program needn't handle non-finite values.
Results may differ from the reference program's by a relative error of at most 0.0003.
Values sent between devices are 32-bit elements; how exact they have to be, the bound alone decides.
No kernel may reach another device: no remote copies, remote signals or barrier semaphores. Data moves between devices by JAX's collectives and lax.ppermute only.
A program may use at most 64 MiB of HBM per device.

```python
import math
import jax
import jax.numpy as jnp
from jax import lax

STATE_BLOCK = 64
SAMPLE_BLOCK = 256
SB_DEV = 64
TILE_DEV = 32
ITERS = 2
BASIS = 32
TEMPS = 16
KB_DEV = 16
SAMPLES = 524288
STATES = 16384
TILES = 16384
N_SAMP = 32
N_STATE = 16


def pattern(key):
    keys = jax.random.split(key, 4)
    raw = jax.random.randint(keys[0], (N_SAMP, N_STATE), 0, TILE_DEV)
    count = 1 + raw * raw // TILE_DEV
    full = jax.random.randint(keys[1], (N_STATE,), 0, N_SAMP)
    count = jnp.where(jnp.arange(N_SAMP)[:, None] == full[None, :], TILE_DEV, count)
    turn = jax.random.randint(keys[2], (N_SAMP, N_STATE, 1), 0, KB_DEV)
    offset = jax.random.randint(keys[3], (N_SAMP, N_STATE, KB_DEV), 0, SB_DEV)
    slot = jnp.arange(TILE_DEV, dtype=jnp.int32)[None, None, :]
    col = (slot + turn) % KB_DEV
    row = (jnp.take_along_axis(offset, col, axis=2) + slot // KB_DEV) % SB_DEV
    live = slot < count[:, :, None]
    rows = jnp.where(live, row, 0).reshape(-1).astype(jnp.int32)
    cols = jnp.where(live, col, KB_DEV).reshape(-1).astype(jnp.int32)
    return (rows, cols)


def draw_tile_rows(key, part):
    rows, cols = pattern(key)
    return rows


def draw_tile_cols(key, part):
    rows, cols = pattern(key)
    return cols


def draw_energies(key, part):
    key = jax.random.fold_in(key, 3)
    keys = jax.random.split(key, 1)
    shape = (TILES, STATE_BLOCK, SAMPLE_BLOCK)
    return 3.0 * jax.random.truncated_normal(keys[0], -6.0, 6.0, shape, jnp.float32)


def place_ends(array, key, low, high):
    spot = [jax.random.randint(jax.random.fold_in(key, axis), (), 0, length) for axis, length in enumerate(array.shape)]
    longest = array.shape.index(max(array.shape))
    next_to = spot[:longest] + [(spot[longest] + 1) % array.shape[longest]] + spot[longest + 1:]
    return array.at[tuple(spot)].set(low).at[tuple(next_to)].set(high)


def block_scale(stream_key, dims, shards, least, high):
    def one(axis_at, shards_of):
        heights = jax.random.uniform(jax.random.fold_in(jax.random.fold_in(stream_key, 6), axis_at), (shards_of,), jnp.float32, least / len(shards), high / len(shards))
        return jnp.repeat(jnp.exp(heights), dims[axis_at] // shards_of).reshape((-1,) + (1,) * (len(dims) - axis_at - 1))

    gain = one(*shards[0])
    for cut in shards[1:]:
        gain = gain * one(*cut)
    return gain


def centred(key, shape, spread, reach, cuts=(), kind=jnp.bfloat16):
    values = jax.random.normal(key, shape, jnp.float32) * spread
    if len(cuts) > 0:
        values = block_scale(key, shape, cuts, -0.22, 0.18) * values
    return jnp.clip(values, min=-reach, max=reach).astype(kind)


def setup_inputs(seed: int = 0) -> dict:
    splits = jax.random.split(jax.random.key(seed), 9)
    energies = draw_energies(jax.random.fold_in(splits[8], 71), 0)
    tile_rows = draw_tile_rows(jax.random.fold_in(splits[8], 71), 0)
    tile_cols = draw_tile_cols(jax.random.fold_in(splits[8], 71), 0)
    start_free = centred(splits[3], (STATES,), 2.0, 8.0, ((0, 16),), jnp.float32)
    temps = place_ends(jax.random.randint(splits[4], (STATES,), 0, TEMPS), jax.random.fold_in(splits[4], 1), 0, TEMPS - 1).astype(jnp.int32)
    betas = jnp.clip(jnp.exp(jax.random.uniform(splits[5], (TEMPS,), jnp.float32, math.log(0.4), math.log(2.5))), 0.4, 2.5)
    counts = place_ends(jax.random.randint(splits[6], (STATES,), 256, 769), jax.random.fold_in(splits[6], 1), 256, 768).astype(jnp.int32)
    basis = centred(splits[7], (BASIS, SAMPLES), 1.0, 6.0, ((1, 32),))
    return dict(energies=energies, tile_rows=tile_rows, tile_cols=tile_cols, start_free=start_free, temps=temps, betas=betas, counts=counts, basis=basis)


NEG = -1.0e30


def reference(energies, tile_rows, tile_cols, start_free, temps, betas, counts, basis):
    groups = N_SAMP * N_STATE
    place = jnp.arange(TILES, dtype=jnp.int32) // TILE_DEV
    live = tile_cols < KB_DEV
    sample_block = ((place // N_STATE) * SB_DEV + tile_rows).astype(jnp.int32)
    state_block = ((place % N_STATE) * KB_DEV + jnp.minimum(tile_cols, KB_DEV - 1)).astype(jnp.int32)
    sample_blocks = N_SAMP * SB_DEV
    state_blocks = N_STATE * KB_DEV
    beta_tile = betas[temps].reshape(-1, STATE_BLOCK)[state_block]
    log_count = jnp.log(counts.astype(jnp.float32))
    blocks = energies.reshape(groups, TILE_DEV, STATE_BLOCK, SAMPLE_BLOCK)
    live_float = live.astype(jnp.float32)

    def split(x):
        return x.reshape((groups, TILE_DEV) + x.shape[1:])

    def score(e, b, bias, lv):
        return jnp.where(lv[:, None, None], bias[:, :, None] - b[:, :, None] * e, NEG)

    def value(e, b, d, lv):
        return jnp.where(lv[:, None, None], -b[:, :, None] * e - d[:, None, :], NEG)

    basis_blocks = basis.reshape(BASIS, sample_blocks, SAMPLE_BLOCK)
    free = start_free
    averages = None
    for step in range(ITERS):
        bias_tile = (log_count + free).reshape(-1, STATE_BLOCK)[state_block]
        pieces = (blocks, split(beta_tile), split(bias_tile), split(live))
        tile_peak = lax.map(lambda a: jnp.max(score(*a), axis=1), pieces).reshape(-1, SAMPLE_BLOCK)
        block_peak = jnp.full((sample_blocks, SAMPLE_BLOCK), NEG, jnp.float32).at[sample_block].max(tile_peak)
        shift = split(block_peak[sample_block])
        tile_total = lax.map(lambda a: jnp.sum(jnp.exp(score(*a[:4]) - a[4][:, None, :]), axis=1), pieces + (shift,)).reshape(-1, SAMPLE_BLOCK)
        block_total = jax.ops.segment_sum(tile_total * live_float[:, None], sample_block, sample_blocks)
        drop = block_peak + jnp.log(jnp.maximum(block_total, 1.0))
        drop_tile = split(drop[sample_block])
        second = (blocks, split(beta_tile), drop_tile, split(live))
        peak_two = lax.map(lambda a: jnp.max(value(*a), axis=2), second).reshape(-1, STATE_BLOCK)
        state_peak = jnp.full((state_blocks, STATE_BLOCK), NEG, jnp.float32).at[state_block].max(peak_two)
        shift_two = split(state_peak[state_block])
        if step + 1 < ITERS:
            totals = lax.map(lambda a: jnp.sum(jnp.exp(value(*a[:4]) - a[4][:, :, None]), axis=2), second + (shift_two,)).reshape(-1, STATE_BLOCK)
            state_total = jax.ops.segment_sum(totals * live_float[:, None], state_block, state_blocks)
            free = -(state_peak + jnp.log(state_total)).reshape(-1)
        else:
            def last(a):
                weight = jnp.exp(value(*a[:4]) - a[4][:, :, None])
                values = basis_blocks[:, a[5]].astype(jnp.float32)
                numer = jnp.einsum("tab,mtb->tma", weight, values, precision=lax.Precision.HIGHEST)
                return jnp.sum(weight, axis=2), numer
            totals, numers = lax.map(last, second + (shift_two, split(sample_block)))
            totals = totals.reshape(-1, STATE_BLOCK)
            numers = numers.reshape(-1, BASIS, STATE_BLOCK)
            state_total = jax.ops.segment_sum(totals * live_float[:, None], state_block, state_blocks)
            state_numer = jax.ops.segment_sum(numers * live_float[:, None, None], state_block, state_blocks)
            state_numer = jnp.transpose(state_numer, (1, 0, 2)).reshape(BASIS, -1)
            averages = state_numer / state_total.reshape(-1)[None, :]
    return averages
```

```python
import jax
import jax.numpy as jnp
from jax import lax
from jax.experimental import pallas as pl
from jax.experimental.pallas import tpu as pltpu
from jax.sharding import PartitionSpec as P

NEG = -1e30
TINY = 1e-30
LANES = 128
UNROLL = 4
F32 = jnp.float32


def vmem(count):
    return [pl.BlockSpec(memory_space=pltpu.VMEM)] * count


def smem(count):
    return [pl.BlockSpec(memory_space=pltpu.SMEM)] * count


def params():
    return pltpu.CompilerParams(vmem_limit_bytes=40 * 1024 * 1024)


def state_beta(temps, betas_ref):
    beta = jnp.zeros(temps.shape, F32)
    for i in range(betas_ref.shape[0]):
        beta = jnp.where(temps == i, betas_ref[i], beta)
    return beta


def expand(rows, cols_ref):
    turned = rows.T
    size = cols_ref.shape[1]
    each = LANES // size
    for j in range(rows.shape[0]):
        wide = jnp.broadcast_to(turned[:, j:j + 1], (LANES, LANES))
        for i in range(each):
            cols_ref[each * j + i] = wide[i * size:(i + 1) * size]
    cols_ref[cols_ref.shape[0] - 1] = jnp.zeros(cols_ref.shape[1:], F32)


def live_groups(cols_ref, blocks):
    live = jnp.int32(0)
    for t in range(cols_ref.shape[0]):
        live = live + (cols_ref[t] < blocks).astype(jnp.int32)
    return (live + UNROLL - 1) // UNROLL


def each_tile(groups, rows_ref, cols_ref, blocks, spare, visit):
    def group(g, carry):
        for i in range(UNROLL):
            t = g * UNROLL + i
            col = cols_ref[t]
            visit(t, jnp.where(col < blocks, rows_ref[t], spare), col)
        return carry

    lax.fori_loop(0, groups, group, 0)


def halves(energies_ref, t):
    count = energies_ref.shape[2] // LANES
    return [energies_ref[t, :, h * LANES:(h + 1) * LANES] for h in range(count)]


def copies(out_ref, value):
    for i in range(out_ref.shape[0]):
        out_ref[i] = value


def first_samples(rows_ref, cols_ref, betas_ref, energies_ref, free_ref, temps_ref, counts_ref, out_ref,
                  beta_cols, bias_cols, peak, total):
    blocks = beta_cols.shape[0] - 1
    blocks_samp = out_ref.shape[1] // peak.shape[0]
    groups = live_groups(cols_ref, blocks)
    expand(state_beta(temps_ref[...], betas_ref), beta_cols)
    expand(jnp.log(counts_ref[...].astype(F32)) + free_ref[...], bias_cols)
    peak[...] = jnp.full(peak.shape, NEG, F32)
    total[...] = jnp.zeros(total.shape, F32)

    def find_peak(t, row, col):
        beta, bias = beta_cols[col], bias_cols[col]
        for h, energy in enumerate(halves(energies_ref, t)):
            top = jnp.max(bias - beta * energy, axis=0, keepdims=True)
            peak[h, pl.ds(row, 1)] = jnp.maximum(peak[h, pl.ds(row, 1)], top)

    def add_up(t, row, col):
        beta, bias = beta_cols[col], bias_cols[col]
        for h, energy in enumerate(halves(energies_ref, t)):
            part = jnp.exp(bias - beta * energy - peak[h, pl.ds(row, 1)])
            total[h, pl.ds(row, 1)] += jnp.sum(part, axis=0, keepdims=True)

    each_tile(groups, rows_ref, cols_ref, blocks, blocks_samp, find_peak)
    each_tile(groups, rows_ref, cols_ref, blocks, blocks_samp, add_up)
    for h in range(peak.shape[0]):
        whole = peak[h, :blocks_samp] + jnp.log(jnp.maximum(total[h, :blocks_samp], 1.0))
        for i in range(out_ref.shape[0]):
            out_ref[i, h * blocks_samp:(h + 1) * blocks_samp] = whole


def load_drop(drop_ref, drop):
    blocks_samp = drop_ref.shape[0] // drop.shape[0]
    for h in range(drop.shape[0]):
        drop[h, :blocks_samp] = drop_ref[h * blocks_samp:(h + 1) * blocks_samp]
        drop[h, blocks_samp:] = jnp.zeros((drop.shape[1] - blocks_samp, LANES), F32)


def first_states(rows_ref, cols_ref, betas_ref, energies_ref, temps_ref, parts_ref, out_ref, drop_ref,
                 beta_cols, drop, top, total):
    blocks = beta_cols.shape[0] - 1
    blocks_samp = drop_ref.shape[0] // drop.shape[0]
    groups = live_groups(cols_ref, blocks)
    expand(state_beta(temps_ref[...], betas_ref), beta_cols)
    peak = jnp.max(parts_ref[...], axis=0)
    whole = jnp.sum(jnp.exp(parts_ref[...] - peak[None]), axis=0)
    drop_ref[...] = peak + jnp.log(jnp.maximum(whole, 1.0))
    load_drop(drop_ref, drop)
    top[...] = jnp.full(top.shape, NEG, F32)
    total[...] = jnp.zeros(total.shape, F32)

    def find_top(t, row, col):
        beta = beta_cols[col]
        for h, energy in enumerate(halves(energies_ref, t)):
            top[col] = jnp.maximum(top[col], -(beta * energy) - drop[h, pl.ds(row, 1)])

    def add_up(t, row, col):
        beta, most = beta_cols[col], top[col]
        part = jnp.zeros(most.shape, F32)
        for h, energy in enumerate(halves(energies_ref, t)):
            part = part + jnp.exp(-(beta * energy) - drop[h, pl.ds(row, 1)] - most)
        total[col] += part

    each_tile(groups, rows_ref, cols_ref, blocks, blocks_samp, find_top)
    for c in range(blocks):
        top[c] = jnp.broadcast_to(jnp.max(top[c], axis=1, keepdims=True), top.shape[1:])
    each_tile(groups, rows_ref, cols_ref, blocks, blocks_samp, add_up)
    each = LANES // top.shape[1]
    lane = lax.broadcasted_iota(jnp.int32, (LANES, LANES), 1)
    turned = jnp.zeros((LANES, LANES), F32)
    for j in range(blocks // each):
        column = [
            top[c] + jnp.log(jnp.maximum(jnp.sum(total[c], axis=1, keepdims=True), 1.0))
            for c in range(each * j, each * j + each)
        ]
        turned = jnp.where(lane == j, jnp.concatenate(column, axis=0), turned)
    copies(out_ref, turned.T[:blocks // each])


def second_samples(rows_ref, cols_ref, betas_ref, energies_ref, temps_ref, counts_ref, drop_ref, parts_ref,
                   out_ref, bias_ref, beta_cols, bias_cols, drop, total):
    blocks = beta_cols.shape[0] - 1
    blocks_samp = drop_ref.shape[0] // drop.shape[0]
    groups = live_groups(cols_ref, blocks)
    top = jnp.max(parts_ref[...], axis=0)
    free = -(top + jnp.log(jnp.sum(jnp.exp(parts_ref[...] - top[None]), axis=0)))
    bias_ref[...] = jnp.log(counts_ref[...].astype(F32)) + free
    expand(state_beta(temps_ref[...], betas_ref), beta_cols)
    expand(bias_ref[...], bias_cols)
    load_drop(drop_ref, drop)
    total[...] = jnp.zeros(total.shape, F32)

    def add_up(t, row, col):
        beta, bias = beta_cols[col], bias_cols[col]
        for h, energy in enumerate(halves(energies_ref, t)):
            part = jnp.exp(bias - beta * energy - drop[h, pl.ds(row, 1)])
            whole = jnp.maximum(jnp.sum(part, axis=0, keepdims=True), jnp.max(part, axis=0, keepdims=True))
            total[h, pl.ds(row, 1)] += whole

    each_tile(groups, rows_ref, cols_ref, blocks, blocks_samp, add_up)
    for h in range(total.shape[0]):
        whole = total[h, :blocks_samp]
        for i in range(out_ref.shape[0]):
            out_ref[i, h * blocks_samp:(h + 1) * blocks_samp] = whole


def second_states(rows_ref, cols_ref, betas_ref, energies_ref, temps_ref, bias_ref, drop_ref, parts_ref, basis_ref,
                  out_ref, beta_cols, bias_cols, drop, values):
    blocks = beta_cols.shape[0] - 1
    blocks_samp = drop_ref.shape[0] // drop.shape[0]
    count = basis_ref.shape[0]
    width = energies_ref.shape[2]
    groups = live_groups(cols_ref, blocks)
    expand(state_beta(temps_ref[...], betas_ref), beta_cols)
    expand(bias_ref[...], bias_cols)
    whole = drop_ref[...] + jnp.log(jnp.maximum(jnp.sum(parts_ref[...], axis=0), TINY))
    for h in range(drop.shape[0]):
        drop[h, :blocks_samp] = whole[h * blocks_samp:(h + 1) * blocks_samp]
        drop[h, blocks_samp:] = jnp.zeros((drop.shape[1] - blocks_samp, LANES), F32)
    values[...] = jnp.zeros(values.shape, F32)
    ones = jnp.ones((values.shape[1] - count, width), jnp.bfloat16)

    def add_up(t, row, col):
        beta, bias = beta_cols[col], bias_cols[col]
        weight = jnp.concatenate(
            [
                jnp.exp(bias - beta * energy - drop[h, pl.ds(row, 1)])
                for h, energy in enumerate(halves(energies_ref, t))
            ],
            axis=1,
        )
        high = weight.astype(jnp.bfloat16)
        low = (weight - high.astype(F32)).astype(jnp.bfloat16)
        start = pl.multiple_of(jnp.minimum(row, blocks_samp - 1) * width, width)
        factor = jnp.concatenate([basis_ref[:, pl.ds(start, width)], ones], axis=0)
        dims = (((1,), (1,)), ((), ()))
        values[col] += lax.dot_general(factor, high, dims, preferred_element_type=F32) + lax.dot_general(
            factor, low, dims, preferred_element_type=F32
        )

    each_tile(groups, rows_ref, cols_ref, blocks, blocks_samp, add_up)
    each = LANES // values.shape[2]
    across = blocks // each
    for j in range(across):
        wide = jnp.concatenate([values[c] for c in range(each * j, each * j + each)], axis=1)
        for g in range(count // 8):
            out_ref[g * across + j, :8] = wide[8 * g:8 * g + 8]
            out_ref[g * across + j, 8:9] = wide[count:count + 1]


def finish(parts_ref, out_ref):
    both = jnp.sum(parts_ref[...], axis=0)
    copies(out_ref, both[:8] / both[8:9])


def spread(parts, axis):
    return lax.all_to_all(parts, axis, 0, 0)


def on_device(n_samp, n_state, energies, tile_rows, tile_cols, start_free, temps, betas, counts, basis):
    slots, state_block, sample_block = energies.shape
    state_dev = start_free.shape[0]
    blocks = state_dev // state_block
    blocks_samp = basis.shape[1] // sample_block
    cut = sample_block // LANES
    rows = state_dev // LANES
    free = start_free.reshape(rows, LANES)
    temps = temps.reshape(rows, LANES)
    counts = counts.reshape(rows, LANES)
    shape = lambda *dims: jax.ShapeDtypeStruct(dims, F32)
    by_state = pltpu.VMEM((blocks + 1, state_block, LANES), F32)
    by_sample = pltpu.VMEM((cut, blocks_samp + 8, LANES), F32)
    parts = pl.pallas_call(
        first_samples,
        out_shape=shape(n_state, cut * blocks_samp, LANES),
        in_specs=smem(3) + vmem(4),
        out_specs=pl.BlockSpec(memory_space=pltpu.VMEM),
        scratch_shapes=[by_state, by_state, by_sample, by_sample],
        compiler_params=params(),
    )(tile_rows, tile_cols, betas, energies, free, temps, counts)
    parts = spread(parts, "state")
    parts, drop = pl.pallas_call(
        first_states,
        out_shape=(shape(n_samp, rows, LANES), shape(cut * blocks_samp, LANES)),
        in_specs=smem(3) + vmem(3),
        out_specs=tuple(vmem(2)),
        scratch_shapes=[by_state, by_sample, by_state, by_state],
        compiler_params=params(),
    )(tile_rows, tile_cols, betas, energies, temps, parts)
    parts = spread(parts, "samp")
    parts, bias = pl.pallas_call(
        second_samples,
        out_shape=(shape(n_state, cut * blocks_samp, LANES), shape(rows, LANES)),
        in_specs=smem(3) + vmem(5),
        out_specs=tuple(vmem(2)),
        scratch_shapes=[by_state, by_state, by_sample, by_sample],
        compiler_params=params(),
    )(tile_rows, tile_cols, betas, energies, temps, counts, drop, parts)
    parts = spread(parts, "state")
    count = basis.shape[0]
    parts = pl.pallas_call(
        second_states,
        out_shape=shape(n_samp, 9, LANES),
        in_specs=smem(3) + vmem(6),
        out_specs=pl.BlockSpec(memory_space=pltpu.VMEM),
        scratch_shapes=[by_state, by_state, by_sample, pltpu.VMEM((blocks + 1, count + 16, state_block), F32)],
        compiler_params=params(),
    )(tile_rows, tile_cols, betas, energies, temps, bias, drop, parts, basis)
    parts = spread(parts, "samp")
    parts = pl.pallas_call(
        finish,
        out_shape=shape(n_samp, 8, LANES),
        in_specs=vmem(1),
        out_specs=pl.BlockSpec(memory_space=pltpu.VMEM),
        compiler_params=params(),
    )(parts)
    parts = spread(parts, "samp")
    return parts.reshape(count // 8, rows, 8, LANES).transpose(0, 2, 1, 3).reshape(count, state_dev)


def solution(mesh):
    n_samp, n_state = mesh.shape["samp"], mesh.shape["state"]

    def run(*args):
        return on_device(n_samp, n_state, *args)

    return jax.shard_map(
        run,
        mesh=mesh,
        in_specs=(
            P(("samp", "state"), None, None),
            P(("samp", "state")),
            P(("samp", "state")),
            P("state"),
            P("state"),
            P(),
            P("state"),
            P(None, "samp"),
        ),
        out_specs=P(None, "state"),
        check_vma=False,
    )
```

```python
import jax
import jax.numpy as jnp
from jax import lax
from jax.experimental import pallas as pl
from jax.experimental.pallas import tpu as pltpu
from jax.sharding import Mesh, PartitionSpec as P

NEG = -1e30
TINY = 1e-30
LANES = 128
UNROLL = 4
F32 = jnp.float32
BF16 = jnp.bfloat16
STEP = 64.0
BASE = -256.0
LAST = 11.0
BITS = 10.0


def vmem(count):
    return [pl.BlockSpec(memory_space=pltpu.VMEM)] * count


def smem(count):
    return [pl.BlockSpec(memory_space=pltpu.SMEM)] * count


def hbm(count):
    return [pl.BlockSpec(memory_space=pltpu.HBM)] * count


def params():
    return pltpu.CompilerParams(vmem_limit_bytes=40 * 1024 * 1024)


def expand(rows, cols_ref):
    turned = rows.T
    size = cols_ref.shape[1]
    each = LANES // size
    for j in range(rows.shape[0]):
        wide = jnp.broadcast_to(turned[:, j:j + 1], (LANES, LANES))
        for i in range(each):
            cols_ref[each * j + i] = wide[i * size:(i + 1) * size]
    cols_ref[cols_ref.shape[0] - 1] = jnp.zeros(cols_ref.shape[1:], F32)


def count_live(cols_ref, blocks):
    live = jnp.int32(0)
    for t in range(cols_ref.shape[0]):
        live = live + (cols_ref[t] < blocks).astype(jnp.int32)
    return live


def each_tile(live, rows_ref, cols_ref, spare, visit):
    def group(g, carry):
        for i in range(UNROLL):
            t = g * UNROLL + i
            visit(t, jnp.where(t < live, rows_ref[t], spare), cols_ref[t])
        return carry

    lax.fori_loop(0, (live + UNROLL - 1) // UNROLL, group, 0)


def halves(energies_ref, t):
    count = energies_ref.shape[2] // LANES
    return [energies_ref[t, :, h * LANES:(h + 1) * LANES] for h in range(count)]


def copies(out_ref, value):
    for i in range(out_ref.shape[0]):
        out_ref[i] = value


def log_sum(parts):
    top = jnp.max(parts, axis=0)
    return top + jnp.log(jnp.sum(jnp.exp(parts - top[None]), axis=0))


def row_sums(hot, values):
    total = None
    for _ in range(3):
        part = values.astype(BF16)
        values = values - part.astype(F32)
        product = jnp.dot(hot, part, preferred_element_type=F32)
        total = product if total is None else total + product
    return total


def by_half(parts_ref, half, slots):
    values = parts_ref[:, half * slots:(half + 1) * slots]
    return values.reshape(values.shape[0] * slots, LANES)


def first_samples(rows_hbm, cols_hbm, betas_hbm, energies_hbm, free_hbm, temps_hbm, counts_hbm,
                  out_ref, beta_ref, count_ref,
                  rows_ref, cols_ref, betas_ref, energies_ref, free_ref, temps_ref, counts_ref,
                  beta_cols, bias_cols, slot, sems):
    blocks = beta_cols.shape[0] - 1
    slots = energies_ref.shape[0]
    cut = energies_ref.shape[2] // LANES
    small = [
        pltpu.make_async_copy(source, target, sems.at[i])
        for i, (source, target) in enumerate([
            (temps_hbm, temps_ref), (counts_hbm, counts_ref), (free_hbm, free_ref),
            (betas_hbm, betas_ref), (cols_hbm, cols_ref), (rows_hbm, rows_ref),
        ])
    ]
    large = [
        pltpu.make_async_copy(
            energies_hbm.at[pl.ds(g * UNROLL, UNROLL)], energies_ref.at[pl.ds(g * UNROLL, UNROLL)],
            sems.at[len(small) + g],
        )
        for g in range(slots // UNROLL)
    ]
    for copy in small + large:
        copy.start()
    for copy in small:
        copy.wait()
    temps = temps_ref[...]
    beta = jnp.zeros(temps.shape, F32)
    for i in range(betas_ref.shape[0]):
        beta = jnp.where(temps == i, betas_ref[i], beta)
    beta_ref[...] = beta
    count_ref[...] = jnp.log(counts_ref[...].astype(F32))
    expand(beta, beta_cols)
    expand(count_ref[...] + free_ref[...], bias_cols)
    live = count_live(cols_ref, blocks)
    slot[...] = jnp.full(slot.shape, NEG, F32)
    lane = lax.broadcasted_iota(jnp.int32, (1, LANES), 1)
    places = jnp.zeros((1, LANES), F32)
    for t in range(slots):
        places = jnp.where(lane == t, rows_ref[t].astype(F32), places)
    slot[cut * slots:cut * slots + 1] = places
    for g in range(slots // UNROLL):
        large[g].wait()

        @pl.when(g * UNROLL < live)
        def _():
            for t in range(g * UNROLL, (g + 1) * UNROLL):
                beta, bias = beta_cols[cols_ref[t]], bias_cols[cols_ref[t]]
                for h, energy in enumerate(halves(energies_ref, t)):
                    score = bias - beta * energy
                    peak = jnp.max(score, axis=0, keepdims=True)
                    total = jnp.sum(jnp.exp(score - peak), axis=0, keepdims=True)
                    whole = peak + jnp.log(jnp.maximum(total, 1.0))
                    slot[h * slots + t:h * slots + t + 1] = jnp.where(t < live, whole, NEG)

    copies(out_ref, slot[...])


def load_drop(value, drop):
    blocks_samp = value.shape[0] // drop.shape[0]
    for h in range(drop.shape[0]):
        drop[h, :blocks_samp] = value[h * blocks_samp:(h + 1) * blocks_samp]
        drop[h, blocks_samp:] = jnp.zeros((drop.shape[1] - blocks_samp, LANES), F32)


def first_states(rows_ref, cols_ref, energies_ref, beta_ref, parts_ref, out_ref, drop_ref, hot_ref,
                 beta_cols, drop, top, total):
    blocks = beta_cols.shape[0] - 1
    cut = drop.shape[0]
    blocks_samp = drop_ref.shape[0] // cut
    slots = energies_ref.shape[0]
    live = count_live(cols_ref, blocks)
    expand(beta_ref[...], beta_cols)
    wide = []
    for j in range(parts_ref.shape[0] * slots // LANES):
        places = jnp.zeros((1, LANES), F32)
        for i in range(LANES // slots):
            place = parts_ref[j * (LANES // slots) + i, cut * slots:cut * slots + 1]
            places = places + (pltpu.roll(place, i * slots, 1) if i else place)
        wide.append(places)
    wide = jnp.concatenate(wide, axis=1)
    row = lax.broadcasted_iota(jnp.int32, (blocks_samp, wide.shape[1]), 0).astype(F32)
    hot = jnp.where(row == wide, 1.0, 0.0).astype(BF16)
    hot_ref[...] = hot
    parts = jnp.concatenate([by_half(parts_ref, h, slots) for h in range(cut)], axis=1)
    step = jnp.clip(jnp.floor((parts - BASE) * (1.0 / STEP)), 0.0, LAST)
    power = jnp.exp2(BITS * step).astype(BF16)
    found = jnp.maximum(jnp.dot(hot, power, preferred_element_type=F32), 1.0)
    step = jnp.floor(jnp.log2(found) * (1.0 / BITS) + 0.03)
    back = lax.dot_general(hot, step.astype(BF16), (((0,), (0,)), ((), ())), preferred_element_type=F32)
    whole = row_sums(hot, jnp.exp(parts - (BASE + STEP * back)))
    whole = BASE + STEP * step + jnp.log(jnp.maximum(whole, 0.5))
    for h in range(cut):
        drop_ref[h * blocks_samp:(h + 1) * blocks_samp] = whole[:, h * LANES:(h + 1) * LANES]
    load_drop(drop_ref[...], drop)
    top[...] = jnp.full(top.shape, NEG, F32)
    total[...] = jnp.zeros(total.shape, F32)

    def find_top(t, row, col):
        beta = beta_cols[col]
        for h, energy in enumerate(halves(energies_ref, t)):
            top[col] = jnp.maximum(top[col], -(beta * energy) - drop[h, pl.ds(row, 1)])

    def add_up(t, row, col):
        beta, most = beta_cols[col], top[col]
        part = jnp.zeros(most.shape, F32)
        for h, energy in enumerate(halves(energies_ref, t)):
            part = part + jnp.exp(-(beta * energy) - drop[h, pl.ds(row, 1)] - most)
        total[col] += part

    each_tile(live, rows_ref, cols_ref, blocks_samp, find_top)
    for c in range(blocks):
        top[c] = jnp.broadcast_to(jnp.max(top[c], axis=1, keepdims=True), top.shape[1:])
    each_tile(live, rows_ref, cols_ref, blocks_samp, add_up)
    each = LANES // top.shape[1]
    lane = lax.broadcasted_iota(jnp.int32, (LANES, LANES), 1)
    turned = jnp.zeros((LANES, LANES), F32)
    for j in range(blocks // each):
        column = [
            top[c] + jnp.log(jnp.maximum(jnp.sum(total[c], axis=1, keepdims=True), 1.0))
            for c in range(each * j, each * j + each)
        ]
        turned = jnp.where(lane == j, jnp.concatenate(column, axis=0), turned)
    out_ref[...] = turned.T[:blocks // each]


def both_cores(parts_ref, out_ref):
    copies(out_ref, log_sum(parts_ref[...]))


def second_samples(rows_ref, cols_ref, energies_ref, beta_ref, count_ref, drop_ref, parts_ref,
                   out_ref, bias_ref, beta_cols, bias_cols, drop, slot):
    blocks = beta_cols.shape[0] - 1
    cut = drop.shape[0]
    blocks_samp = drop_ref.shape[0] // cut
    slots = energies_ref.shape[0]
    live = count_live(cols_ref, blocks)
    bias_ref[...] = count_ref[...] - log_sum(parts_ref[...])
    expand(beta_ref[...], beta_cols)
    expand(bias_ref[...], bias_cols)
    load_drop(drop_ref[...], drop)
    slot[...] = jnp.zeros(slot.shape, F32)
    for g in range(slots // UNROLL):

        @pl.when(g * UNROLL < live)
        def _():
            for t in range(g * UNROLL, (g + 1) * UNROLL):
                beta, bias = beta_cols[cols_ref[t]], bias_cols[cols_ref[t]]
                for h, energy in enumerate(halves(energies_ref, t)):
                    part = jnp.exp(bias - beta * energy - drop[h, pl.ds(rows_ref[t], 1)])
                    whole = jnp.maximum(jnp.sum(part, axis=0, keepdims=True), jnp.max(part, axis=0, keepdims=True))
                    slot[h * slots + t:h * slots + t + 1] = jnp.where(t < live, whole, 0.0)

    copies(out_ref, slot[...])


def second_states(rows_ref, cols_ref, energies_ref, beta_ref, bias_ref, drop_ref, hot_ref, parts_ref, basis_ref,
                  out_ref, beta_cols, bias_cols, drop, values):
    blocks = beta_cols.shape[0] - 1
    cut = drop.shape[0]
    blocks_samp = drop_ref.shape[0] // cut
    slots = energies_ref.shape[0]
    count = basis_ref.shape[0]
    width = energies_ref.shape[2]
    live = count_live(cols_ref, blocks)
    expand(beta_ref[...], beta_cols)
    expand(bias_ref[...], bias_cols)
    parts = jnp.concatenate([by_half(parts_ref, h, slots) for h in range(cut)], axis=1)
    whole = jnp.log(jnp.maximum(row_sums(hot_ref[...], parts), TINY))
    whole = jnp.concatenate([whole[:, h * LANES:(h + 1) * LANES] for h in range(cut)], axis=0)
    load_drop(drop_ref[...] + whole, drop)
    values[...] = jnp.zeros(values.shape, F32)
    ones = jnp.ones((values.shape[1] - count, width), BF16)

    def add_up(t, row, col):
        beta, bias = beta_cols[col], bias_cols[col]
        weight = jnp.concatenate(
            [
                jnp.exp(bias - beta * energy - drop[h, pl.ds(row, 1)])
                for h, energy in enumerate(halves(energies_ref, t))
            ],
            axis=1,
        )
        high = weight.astype(BF16)
        low = (weight - high.astype(F32)).astype(BF16)
        start = pl.multiple_of(jnp.minimum(row, blocks_samp - 1) * width, width)
        factor = jnp.concatenate([basis_ref[:, pl.ds(start, width)], ones], axis=0)
        dims = (((1,), (1,)), ((), ()))
        values[col] += lax.dot_general(factor, high, dims, preferred_element_type=F32) + lax.dot_general(
            factor, low, dims, preferred_element_type=F32
        )

    each_tile(live, rows_ref, cols_ref, blocks_samp, add_up)
    each = LANES // values.shape[2]
    across = blocks // each
    half = out_ref.shape[1]
    for j in range(across):
        wide = jnp.concatenate([values[c] for c in range(each * j, each * j + each)], axis=1)
        for g in range(count // 8):
            owner = g * across + j
            for r in range(8):
                out_ref[owner // half, owner % half, r] = wide[8 * g + r:8 * g + r + 1]
            out_ref[owner // half, owner % half, 8] = wide[count:count + 1]


def core_sums(parts_ref, out_ref):
    mine = lax.axis_index("core")
    out_ref[...] = parts_ref[0, mine] + parts_ref[1, mine]


def finish(parts_ref, out_ref):
    both = jnp.sum(parts_ref[...], axis=0)
    value = jnp.concatenate([both[r] for r in range(8)], axis=0)
    copies(out_ref, value / both[8])


def spread(parts, axis):
    return lax.all_to_all(parts, axis, 0, 0)


def call(kernel, out_shape, in_specs, scratch_shapes=()):
    single = not isinstance(out_shape, tuple)
    return pl.pallas_call(
        kernel,
        out_shape=out_shape,
        in_specs=in_specs,
        out_specs=vmem(1)[0] if single else tuple(vmem(len(out_shape))),
        scratch_shapes=list(scratch_shapes),
        compiler_params=params(),
    )


def on_device(n_core, n_z, n_state, energies, tile_rows, tile_cols, start_free, temps, betas, counts, basis):
    slots, state_block, sample_block = energies.shape
    state_dev = start_free.shape[0]
    blocks = state_dev // state_block
    blocks_samp = basis.shape[1] // sample_block
    cut = sample_block // LANES
    rows = state_dev // LANES
    count = basis.shape[0]
    shape = lambda *dims: jax.ShapeDtypeStruct(dims, F32)
    by_state = pltpu.VMEM((blocks + 1, state_block, LANES), F32)
    by_sample = pltpu.VMEM((cut, blocks_samp + 8, LANES), F32)
    flat = pltpu.VMEM((rows, LANES), F32)
    whole = pltpu.VMEM((rows, LANES), jnp.int32)

    parts, beta, log_count = call(
        first_samples,
        (shape(n_state, cut * slots + 8, LANES), shape(rows, LANES), shape(rows, LANES)),
        hbm(7),
        [
            pltpu.SMEM(tile_rows.shape, jnp.int32),
            pltpu.SMEM(tile_cols.shape, jnp.int32),
            pltpu.SMEM(betas.shape, F32),
            pltpu.VMEM(energies.shape, F32),
            flat, whole, whole, by_state, by_state,
            pltpu.VMEM((cut * slots + 8, LANES), F32),
            pltpu.SemaphoreType.DMA((6 + slots // UNROLL,)),
        ],
    )(
        tile_rows, tile_cols, betas, energies,
        start_free.reshape(rows, LANES), temps.reshape(rows, LANES), counts.reshape(rows, LANES),
    )
    parts = spread(parts, "state")
    parts, drop, hot = call(
        first_states,
        (
            shape(rows, LANES), shape(cut * blocks_samp, LANES),
            jax.ShapeDtypeStruct((blocks_samp, n_state * slots), BF16),
        ),
        smem(2) + vmem(3),
        [by_state, by_sample, by_state, by_state],
    )(tile_rows, tile_cols, energies, beta, parts)
    parts = lax.all_gather(parts, "core")
    parts = call(both_cores, shape(n_z, rows, LANES), vmem(1))(parts)
    parts = spread(parts, "z")
    parts, bias = call(
        second_samples,
        (shape(n_state, cut * slots, LANES), shape(rows, LANES)),
        smem(2) + vmem(5),
        [by_state, by_state, by_sample, pltpu.VMEM((cut * slots, LANES), F32)],
    )(tile_rows, tile_cols, energies, beta, log_count, drop, parts)
    parts = spread(parts, "state")
    parts = call(
        second_states,
        shape(n_core, n_z, 9, 1, LANES),
        smem(2) + vmem(7),
        [by_state, by_state, by_sample, pltpu.VMEM((blocks + 1, count + 16, state_block), F32)],
    )(tile_rows, tile_cols, energies, beta, bias, drop, hot, parts, basis)
    parts = lax.all_gather(parts, "core")
    parts = call(core_sums, shape(n_z, 9, 1, LANES), vmem(1))(parts)
    parts = spread(parts, "z")
    parts = call(finish, shape(n_z, 8, LANES), vmem(1))(parts)
    parts = spread(parts, "z")
    parts = lax.all_gather(parts, "core")
    return parts.reshape(count // 8, rows, 8, LANES).transpose(0, 2, 1, 3).reshape(count, state_dev)


def solution(mesh):
    n_samp, n_state = mesh.shape["samp"], mesh.shape["state"]
    n_core = 2
    n_z = n_samp // n_core
    cut = Mesh(mesh.devices.reshape(n_z, n_core, n_state), ("z", "core", "state"))
    samp = ("z", "core")

    def run(*args):
        return on_device(n_core, n_z, n_state, *args)

    return jax.shard_map(
        run,
        mesh=cut,
        in_specs=(
            P(("z", "core", "state"), None, None),
            P(("z", "core", "state")),
            P(("z", "core", "state")),
            P("state"),
            P("state"),
            P(),
            P("state"),
            P(None, samp),
        ),
        out_specs=P(None, "state"),
        check_vma=False,
    )
```

```python
import jax
import jax.numpy as jnp
from jax import lax
from jax.experimental import pallas as pl
from jax.experimental.pallas import tpu as pltpu
from jax.sharding import Mesh, PartitionSpec as P

NEG = -1e30
TINY = 1e-30
LANES = 128
UNROLL = 4
MIB = 1024 * 1024
FIRST_VMEM = 60 * MIB
F32 = jnp.float32
BF16 = jnp.bfloat16
LOG2E = 1.4426950408889634
STEP = 96.0
BASE = -400.0
LAST = 11.0
BITS = 10.0


def vmem(count):
    return [pl.BlockSpec(memory_space=pltpu.VMEM)] * count


def smem(count):
    return [pl.BlockSpec(memory_space=pltpu.SMEM)] * count


def hbm(count):
    return [pl.BlockSpec(memory_space=pltpu.HBM)] * count


def anywhere(count):
    return [pl.BlockSpec(memory_space=pl.ANY)] * count


def expand(rows, cols_ref, spare):
    turned = rows.T
    size = cols_ref.shape[1]
    each = LANES // size
    for j in range(rows.shape[0]):
        wide = jnp.broadcast_to(turned[:, j:j + 1], (LANES, LANES))
        for i in range(each):
            cols_ref[each * j + i] = wide[i * size:(i + 1) * size]
    cols_ref[cols_ref.shape[0] - 1] = jnp.full(cols_ref.shape[1:], spare, F32)


def halves(energies_ref, t):
    count = energies_ref.shape[2] // LANES
    return [energies_ref[t, :, h * LANES:(h + 1) * LANES] for h in range(count)]


def copies(out_ref, value):
    for i in range(out_ref.shape[0]):
        out_ref[i] = value


def log_sum(parts):
    top = jnp.max(parts, axis=0)
    return top + jnp.log2(jnp.sum(jnp.exp2(parts - top[None]), axis=0))


def row_sums(hot, values):
    total = None
    for _ in range(3):
        part = values.astype(BF16)
        values = values - part.astype(F32)
        product = jnp.dot(hot, part, preferred_element_type=F32)
        total = product if total is None else total + product
    return total


def by_half(parts_ref, half, slots):
    values = parts_ref[:, half * slots:(half + 1) * slots]
    return values.reshape(values.shape[0] * slots, LANES)


def first_samples(rows_hbm, cols_hbm, betas_hbm, energies_hbm, free_hbm, temps_hbm, counts_hbm,
                  out_ref, beta_ref, count_ref,
                  rows_ref, cols_ref, betas_ref, energies_ref, free_ref, temps_ref, counts_ref,
                  beta_cols, bias_cols, slot, total, sems):
    slots = energies_ref.shape[0]
    cut = energies_ref.shape[2] // LANES
    small = [
        pltpu.make_async_copy(source, target, sems.at[i])
        for i, (source, target) in enumerate([
            (temps_hbm, temps_ref), (counts_hbm, counts_ref), (free_hbm, free_ref),
            (betas_hbm, betas_ref), (cols_hbm, cols_ref), (rows_hbm, rows_ref),
        ])
    ]
    large = [
        pltpu.make_async_copy(
            energies_hbm.at[pl.ds(g * UNROLL, UNROLL)], energies_ref.at[pl.ds(g * UNROLL, UNROLL)],
            sems.at[len(small) + g],
        )
        for g in range(slots // UNROLL)
    ]
    for copy in small + large:
        copy.start()
    for copy in small:
        copy.wait()
    temps = temps_ref[...]
    beta = jnp.zeros(temps.shape, F32)
    for i in range(betas_ref.shape[0]):
        beta = jnp.where(temps == i, betas_ref[i], beta)
    count_ref[...] = LOG2E * jnp.log(counts_ref[...].astype(F32))
    beta_ref[...] = LOG2E * beta
    expand(beta_ref[...], beta_cols, 0.0)
    expand(count_ref[...] + LOG2E * free_ref[...], bias_cols, NEG)
    lane = lax.broadcasted_iota(jnp.int32, (1, LANES), 1)
    places = jnp.zeros((1, LANES), F32)
    for t in range(slots):
        places = jnp.where(lane == t, rows_ref[t].astype(F32), places)
    for g in range(slots // UNROLL):
        large[g].wait()
        for t in range(g * UNROLL, (g + 1) * UNROLL):
            beta, bias = beta_cols[cols_ref[t]], bias_cols[cols_ref[t]]
            for h, energy in enumerate(halves(energies_ref, t)):
                score = bias - beta * energy
                peak = jnp.max(score, axis=0, keepdims=True)
                slot[h * slots + t:h * slots + t + 1] = peak
                total[h * slots + t:h * slots + t + 1] = jnp.sum(jnp.exp2(score - peak), axis=0, keepdims=True)
    whole = slot[...] + jnp.log2(jnp.maximum(total[...], 1.0))
    for i in range(out_ref.shape[0]):
        out_ref[i, :cut * slots] = whole
        out_ref[i, cut * slots:] = jnp.broadcast_to(places, (8, LANES))


def first_states(rows_hbm, cols_hbm, beta_hbm, energies_ref, parts_ref, out_ref, drop_ref, hot_ref, beta_cols,
                 rows_ref, cols_ref, sems, beta_ref, top, total):
    index = [
        pltpu.make_async_copy(rows_hbm, rows_ref, sems.at[0]), pltpu.make_async_copy(cols_hbm, cols_ref, sems.at[1]),
        pltpu.make_async_copy(beta_hbm, beta_ref, sems.at[2]),
    ]
    for copy in index:
        copy.start()
    blocks = beta_cols.shape[0] - 1
    slots = energies_ref.shape[0]
    cut = energies_ref.shape[2] // LANES
    blocks_samp = drop_ref.shape[0] // cut
    wide = []
    for j in range(parts_ref.shape[0] * slots // LANES):
        places = jnp.zeros((1, LANES), F32)
        for i in range(LANES // slots):
            place = parts_ref[j * (LANES // slots) + i, cut * slots:cut * slots + 1]
            place = jnp.where(lax.broadcasted_iota(jnp.int32, place.shape, 1) < slots, place, 0.0)
            places = places + (pltpu.roll(place, i * slots, 1) if i else place)
        wide.append(places)
    wide = jnp.concatenate(wide, axis=1)
    row = lax.broadcasted_iota(jnp.int32, (blocks_samp, wide.shape[1]), 0).astype(F32)
    hot = jnp.where(row == wide, 1.0, 0.0).astype(BF16)
    hot_ref[...] = hot
    parts = jnp.concatenate([by_half(parts_ref, h, slots) for h in range(cut)], axis=1)
    step = jnp.clip(jnp.floor((parts - BASE) * (1.0 / STEP)), 0.0, LAST)
    power = jnp.exp2(BITS * step).astype(BF16)
    found = jnp.maximum(jnp.dot(hot, power, preferred_element_type=F32), 1.0)
    step = jnp.floor(jnp.log2(found) * (1.0 / BITS) + 0.03)
    back = lax.dot_general(hot, step.astype(BF16), (((0,), (0,)), ((), ())), preferred_element_type=F32)
    whole = row_sums(hot, jnp.exp2(parts - (BASE + STEP * back)))
    whole = BASE + STEP * step + jnp.log2(jnp.maximum(whole, 0.5))
    for h in range(cut):
        drop_ref[h * blocks_samp:(h + 1) * blocks_samp] = whole[:, h * LANES:(h + 1) * LANES]
    top[...] = jnp.full(top.shape, NEG, F32)
    total[...] = jnp.zeros(total.shape, F32)
    for copy in index:
        copy.wait()
    expand(beta_ref[...], beta_cols, 0.0)

    def drop_of(h, t):
        return drop_ref[pl.ds(h * blocks_samp + rows_ref[t], 1)]

    for t in range(slots):
        col = cols_ref[t]
        beta = beta_cols[col]
        most = top[col]
        for h, energy in enumerate(halves(energies_ref, t)):
            most = jnp.maximum(most, -(beta * energy) - drop_of(h, t))
        top[col] = most
    for c in range(blocks):
        top[c] = jnp.broadcast_to(jnp.max(top[c], axis=1, keepdims=True), top.shape[1:])
    for t in range(slots):
        col = cols_ref[t]
        beta, most = beta_cols[col], top[col]
        part = total[col]
        for h, energy in enumerate(halves(energies_ref, t)):
            part = part + jnp.exp2(-(beta * energy) - drop_of(h, t) - most)
        total[col] = part
    each = LANES // top.shape[1]
    lane = lax.broadcasted_iota(jnp.int32, (LANES, LANES), 1)
    tops = jnp.zeros((LANES, LANES), F32)
    sums = jnp.ones((LANES, LANES), F32)
    for j in range(blocks // each):
        column = range(each * j, each * j + each)
        tops = jnp.where(lane == j, jnp.concatenate([top[c] for c in column], axis=0), tops)
        sums = jnp.where(
            lane == j,
            jnp.concatenate([jnp.sum(total[c], axis=1, keepdims=True) for c in column], axis=0),
            sums,
        )
    rows = blocks // each
    out_ref[...] = tops.T[:rows] + jnp.log2(jnp.maximum(sums.T[:rows], 1.0))


def both_cores(parts_ref, out_ref):
    copies(out_ref, log_sum(parts_ref[...]))


def second_samples(rows_hbm, cols_hbm, energies_ref, beta_cols, count_ref, drop_ref, parts_ref,
                   out_ref, bias_cols, rows_ref, cols_ref, sems, slot):
    index = [
        pltpu.make_async_copy(rows_hbm, rows_ref, sems.at[0]), pltpu.make_async_copy(cols_hbm, cols_ref, sems.at[1])
    ]
    for copy in index:
        copy.start()
    slots = energies_ref.shape[0]
    cut = energies_ref.shape[2] // LANES
    blocks_samp = drop_ref.shape[0] // cut
    expand(count_ref[...] - log_sum(parts_ref[...]), bias_cols, NEG)
    for copy in index:
        copy.wait()
    for t in range(slots):
        beta, bias = beta_cols[cols_ref[t]], bias_cols[cols_ref[t]]
        for h, energy in enumerate(halves(energies_ref, t)):
            part = jnp.exp2(bias - beta * energy - drop_ref[pl.ds(h * blocks_samp + rows_ref[t], 1)])
            slot[h * slots + t:h * slots + t + 1] = jnp.maximum(
                jnp.sum(part, axis=0, keepdims=True), jnp.max(part, axis=0, keepdims=True)
            )
    copies(out_ref, slot[...])


def second_states(rows_hbm, cols_hbm, energies_ref, beta_cols, bias_cols, drop_ref, hot_ref, parts_ref, basis_ref,
                  out_ref, rows_ref, cols_ref, sems, drop, values):
    index = [
        pltpu.make_async_copy(rows_hbm, rows_ref, sems.at[0]), pltpu.make_async_copy(cols_hbm, cols_ref, sems.at[1])
    ]
    for copy in index:
        copy.start()
    blocks = beta_cols.shape[0] - 1
    slots = energies_ref.shape[0]
    count = basis_ref.shape[0]
    width = energies_ref.shape[2]
    cut = width // LANES
    blocks_samp = drop_ref.shape[0] // cut
    parts = jnp.concatenate([by_half(parts_ref, h, slots) for h in range(cut)], axis=1)
    whole = jnp.log2(jnp.maximum(row_sums(hot_ref[...], parts), TINY))
    for h in range(cut):
        here = slice(h * blocks_samp, (h + 1) * blocks_samp)
        drop[here] = drop_ref[here] + whole[:, h * LANES:(h + 1) * LANES]
    values[...] = jnp.zeros(values.shape, F32)
    ones = jnp.ones((values.shape[1] - count, width), BF16)
    for copy in index:
        copy.wait()
    for t in range(slots):
        row, col = rows_ref[t], cols_ref[t]
        beta, bias = beta_cols[col], bias_cols[col]
        weight = jnp.concatenate(
            [
                jnp.exp2(bias - beta * energy - drop[pl.ds(h * blocks_samp + row, 1)])
                for h, energy in enumerate(halves(energies_ref, t))
            ],
            axis=1,
        )
        high = weight.astype(BF16)
        low = (weight - high.astype(F32)).astype(BF16)
        factor = jnp.concatenate([basis_ref[:, pl.ds(pl.multiple_of(row * width, width), width)], ones], axis=0)
        dims = (((1,), (1,)), ((), ()))
        values[col] += lax.dot_general(factor, high, dims, preferred_element_type=F32) + lax.dot_general(
            factor, low, dims, preferred_element_type=F32
        )
    each = LANES // values.shape[2]
    across = blocks // each
    half = out_ref.shape[1] // 9
    for j in range(across):
        wide = jnp.concatenate([values[c] for c in range(each * j, each * j + each)], axis=1)
        for g in range(count // 8):
            owner = g * across + j
            start = owner % half * 9
            out_ref[owner // half, start:start + 8] = wide[8 * g:8 * g + 8]
            out_ref[owner // half, start + 8:start + 9] = wide[count:count + 1]


def core_sums(parts_ref, out_ref):
    mine = my_core()
    value = parts_ref[0, mine] + parts_ref[1, mine]
    for i in range(out_ref.shape[0]):
        for r in range(9):
            out_ref[i, r] = value[9 * i + r:9 * i + r + 1]


def finish(parts_ref, out_ref):
    both = jnp.sum(parts_ref[...], axis=0)
    value = jnp.concatenate([both[r] for r in range(8)], axis=0)
    copies(out_ref, value / both[8])


def spread(parts, axis):
    return lax.all_to_all(parts, axis, 0, 0)


def pair(parts):
    return lax.all_gather(parts, "core")


def my_core():
    return lax.axis_index("core")


def call(kernel, out_shape, in_specs, scratch_shapes=(), limit=40 * MIB):
    single = not isinstance(out_shape, tuple)
    return pl.pallas_call(
        kernel,
        out_shape=out_shape,
        in_specs=in_specs,
        out_specs=vmem(1)[0] if single else tuple(vmem(len(out_shape))),
        scratch_shapes=list(scratch_shapes),
        compiler_params=pltpu.CompilerParams(vmem_limit_bytes=limit),
    )


def on_device(n_core, n_z, n_state, energies, tile_rows, tile_cols, start_free, temps, betas, counts, basis):
    slots, state_block, sample_block = energies.shape
    state_dev = start_free.shape[0]
    blocks = state_dev // state_block
    blocks_samp = basis.shape[1] // sample_block
    cut = sample_block // LANES
    rows = state_dev // LANES
    count = basis.shape[0]
    shape = lambda *dims: jax.ShapeDtypeStruct(dims, F32)
    by_state = (blocks + 1, state_block, LANES)
    place = [
        pltpu.SMEM(tile_rows.shape, jnp.int32), pltpu.SMEM(tile_cols.shape, jnp.int32), pltpu.SemaphoreType.DMA((3,))
    ]
    flat = pltpu.VMEM((rows, LANES), F32)
    whole = pltpu.VMEM((rows, LANES), jnp.int32)
    by_slot = pltpu.VMEM((cut * slots, LANES), F32)

    parts, beta, log_count = call(
        first_samples,
        (shape(n_state, cut * slots + 8, LANES), shape(rows, LANES), shape(rows, LANES)),
        hbm(7),
        place[:2] + [
            pltpu.SMEM(betas.shape, F32),
            pltpu.VMEM(energies.shape, F32),
            flat, whole, whole, pltpu.VMEM(by_state, F32), pltpu.VMEM(by_state, F32), by_slot, by_slot,
            pltpu.SemaphoreType.DMA((6 + slots // UNROLL,)),
        ],
        FIRST_VMEM,
    )(
        tile_rows, tile_cols, betas, energies,
        start_free.reshape(rows, LANES), temps.reshape(rows, LANES), counts.reshape(rows, LANES),
    )
    parts = spread(parts, "state")
    parts, drop, hot, beta_cols = call(
        first_states,
        (
            shape(rows, LANES), shape(cut * blocks_samp, LANES),
            jax.ShapeDtypeStruct((blocks_samp, n_state * slots), BF16), shape(*by_state),
        ),
        anywhere(3) + vmem(2),
        place + [flat, pltpu.VMEM(by_state, F32), pltpu.VMEM(by_state, F32)],
    )(tile_rows, tile_cols, beta, energies, parts)
    parts = pair(parts)
    parts = call(both_cores, shape(n_z, rows, LANES), vmem(1))(parts)
    parts = spread(parts, "z")
    parts, bias = call(
        second_samples,
        (shape(n_state, cut * slots, LANES), shape(*by_state)),
        anywhere(2) + vmem(5),
        place + [by_slot],
    )(tile_rows, tile_cols, energies, beta_cols, log_count, drop, parts)
    parts = spread(parts, "state")
    parts = call(
        second_states,
        shape(n_core, n_z * 9, LANES),
        anywhere(2) + vmem(7),
        place + [
            pltpu.VMEM((cut * blocks_samp, LANES), F32), pltpu.VMEM((blocks + 1, count + 16, state_block), F32)
        ],
    )(tile_rows, tile_cols, energies, beta_cols, bias, drop, hot, parts, basis)
    parts = pair(parts)
    parts = call(core_sums, shape(n_z, 9, 1, LANES), vmem(1))(parts)
    parts = spread(parts, "z")
    parts = call(finish, shape(n_z, 8, LANES), vmem(1))(parts)
    parts = spread(parts, "z")
    parts = pair(parts)
    return parts.reshape(count // 8, rows, 8, LANES).transpose(0, 2, 1, 3).reshape(count, state_dev)


def solution(mesh):
    n_samp, n_state = mesh.shape["samp"], mesh.shape["state"]
    n_core = 2
    n_z = n_samp // n_core
    cut = Mesh(mesh.devices.reshape(n_z, n_core, n_state), ("z", "core", "state"))
    samp = ("z", "core")

    def run(*args):
        return on_device(n_core, n_z, n_state, *args)

    return jax.shard_map(
        run,
        mesh=cut,
        in_specs=(
            P(("z", "core", "state"), None, None),
            P(("z", "core", "state")),
            P(("z", "core", "state")),
            P("state"),
            P("state"),
            P(),
            P("state"),
            P(None, samp),
        ),
        out_specs=P(None, "state"),
        check_vma=False,
    )
```

```python
import jax
import jax.numpy as jnp
from jax import lax
from jax.experimental import pallas as pl
from jax.experimental.pallas import tpu as pltpu
from jax.sharding import Mesh, PartitionSpec as P

NEG = -1e30
TINY = 1e-30
LANES = 128
UNROLL = 4
MIB = 1024 * 1024
FIRST_VMEM = 60 * MIB
F32 = jnp.float32
BF16 = jnp.bfloat16
LOG2E = 1.4426950408889634
STEP = 96.0
BASE = -400.0
LAST = 11.0
BITS = 10.0


def vmem(count):
    return [pl.BlockSpec(memory_space=pltpu.VMEM)] * count


def smem(count):
    return [pl.BlockSpec(memory_space=pltpu.SMEM)] * count


def hbm(count):
    return [pl.BlockSpec(memory_space=pltpu.HBM)] * count


def anywhere(count):
    return [pl.BlockSpec(memory_space=pl.ANY)] * count


def state_beta(temps, betas_ref):
    beta = jnp.zeros(temps.shape, F32)
    for i in range(betas_ref.shape[0]):
        beta = jnp.where(temps == i, betas_ref[i], beta)
    return -LOG2E * beta


def log_count(counts_ref):
    return LOG2E * jnp.log(counts_ref[...].astype(F32))


def expand(rows, cols_ref, spare):
    turned = rows.T
    size = cols_ref.shape[1]
    each = LANES // size
    for j in range(rows.shape[0]):
        wide = jnp.broadcast_to(turned[:, j:j + 1], (LANES, LANES))
        for i in range(each):
            cols_ref[each * j + i] = wide[i * size:(i + 1) * size]
    cols_ref[cols_ref.shape[0] - 1] = jnp.full(cols_ref.shape[1:], spare, F32)


def halves(energies_ref, t):
    count = energies_ref.shape[2] // LANES
    return [energies_ref[t, :, h * LANES:(h + 1) * LANES] for h in range(count)]


def copies(out_ref, value):
    for i in range(out_ref.shape[0]):
        out_ref[i] = value


def log_sum(parts):
    top = jnp.max(parts, axis=0)
    return top + jnp.log2(jnp.sum(jnp.exp2(parts - top[None]), axis=0))


def row_sums(hot, values):
    total = None
    for _ in range(3):
        part = values.astype(BF16)
        values = values - part.astype(F32)
        product = jnp.dot(hot, part, preferred_element_type=F32)
        total = product if total is None else total + product
    return total


def by_half(parts_ref, half, slots):
    values = parts_ref[:, half * slots:(half + 1) * slots]
    return values.reshape(values.shape[0] * slots, LANES)


def first_samples(rows_hbm, cols_hbm, betas_hbm, energies_hbm, free_hbm, temps_hbm, counts_hbm,
                  out_ref,
                  rows_ref, cols_ref, betas_ref, energies_ref, free_ref, temps_ref, counts_ref,
                  beta_cols, bias_cols, slot, total, sems):
    slots = energies_ref.shape[0]
    cut = energies_ref.shape[2] // LANES
    small = [
        pltpu.make_async_copy(source, target, sems.at[i])
        for i, (source, target) in enumerate([
            (temps_hbm, temps_ref), (counts_hbm, counts_ref), (free_hbm, free_ref),
            (betas_hbm, betas_ref), (cols_hbm, cols_ref), (rows_hbm, rows_ref),
        ])
    ]
    large = [
        pltpu.make_async_copy(
            energies_hbm.at[pl.ds(g * UNROLL, UNROLL)], energies_ref.at[pl.ds(g * UNROLL, UNROLL)],
            sems.at[len(small) + g],
        )
        for g in range(slots // UNROLL)
    ]
    for copy in small + large:
        copy.start()
    for copy in small:
        copy.wait()
    expand(state_beta(temps_ref[...], betas_ref), beta_cols, 0.0)
    expand(log_count(counts_ref) + LOG2E * free_ref[...], bias_cols, NEG)
    lane = lax.broadcasted_iota(jnp.int32, (1, LANES), 1)
    places = jnp.zeros((1, LANES), F32)
    for t in range(slots):
        places = jnp.where(lane == t, rows_ref[t].astype(F32), places)
    for g in range(slots // UNROLL):
        large[g].wait()
        for t in range(g * UNROLL, (g + 1) * UNROLL):
            beta, bias = beta_cols[cols_ref[t]], bias_cols[cols_ref[t]]
            for h, energy in enumerate(halves(energies_ref, t)):
                score = bias + beta * energy
                peak = jnp.max(score, axis=0, keepdims=True)
                slot[h * slots + t:h * slots + t + 1] = peak
                total[h * slots + t:h * slots + t + 1] = jnp.sum(jnp.exp2(score - peak), axis=0, keepdims=True)
    whole = slot[...] + jnp.log2(jnp.maximum(total[...], 1.0))
    for i in range(out_ref.shape[0]):
        out_ref[i, :cut * slots] = whole
        out_ref[i, cut * slots:] = jnp.broadcast_to(places, (8, LANES))


def first_states(rows_hbm, cols_hbm, betas_hbm, temps_ref, energies_ref, parts_ref, out_ref, values_ref, hot_ref,
                 rows_ref, cols_ref, sems, betas_ref, beta_cols, drop, top, total):
    index = [
        pltpu.make_async_copy(rows_hbm, rows_ref, sems.at[0]), pltpu.make_async_copy(cols_hbm, cols_ref, sems.at[1]),
        pltpu.make_async_copy(betas_hbm, betas_ref, sems.at[2]),
    ]
    for copy in index:
        copy.start()
    blocks = beta_cols.shape[0] - 1
    slots = energies_ref.shape[0]
    cut = energies_ref.shape[2] // LANES
    blocks_samp = drop.shape[0] // cut
    wide = []
    for j in range(parts_ref.shape[0] * slots // LANES):
        places = jnp.zeros((1, LANES), F32)
        for i in range(LANES // slots):
            place = parts_ref[j * (LANES // slots) + i, cut * slots:cut * slots + 1]
            place = jnp.where(lax.broadcasted_iota(jnp.int32, place.shape, 1) < slots, place, 0.0)
            places = places + (pltpu.roll(place, i * slots, 1) if i else place)
        wide.append(places)
    wide = jnp.concatenate(wide, axis=1)
    row = lax.broadcasted_iota(jnp.int32, (blocks_samp, wide.shape[1]), 0).astype(F32)
    hot = jnp.where(row == wide, 1.0, 0.0).astype(BF16)
    hot_ref[...] = hot
    parts = jnp.concatenate([by_half(parts_ref, h, slots) for h in range(cut)], axis=1)
    step = jnp.clip(jnp.floor((parts - BASE) * (1.0 / STEP)), 0.0, LAST)
    power = jnp.exp2(BITS * step).astype(BF16)
    found = jnp.maximum(jnp.dot(hot, power, preferred_element_type=F32), 1.0)
    step = jnp.floor(jnp.log2(found) * (1.0 / BITS) + 0.03)
    back = lax.dot_general(hot, step.astype(BF16), (((0,), (0,)), ((), ())), preferred_element_type=F32)
    whole = row_sums(hot, jnp.exp2(parts - (BASE + STEP * back)))
    whole = BASE + STEP * step + jnp.log2(jnp.maximum(whole, 0.5))
    for h in range(cut):
        drop[h * blocks_samp:(h + 1) * blocks_samp] = whole[:, h * LANES:(h + 1) * LANES]
    top[...] = jnp.full(top.shape, NEG, F32)
    total[...] = jnp.zeros(total.shape, F32)
    for copy in index:
        copy.wait()
    expand(state_beta(temps_ref[...], betas_ref), beta_cols, 0.0)

    for t in range(slots):
        row, col = rows_ref[t], cols_ref[t]
        beta = beta_cols[col]
        most = top[col]
        for h, energy in enumerate(halves(energies_ref, t)):
            value = beta * energy - drop[pl.ds(h * blocks_samp + row, 1)]
            values_ref[t, :, h * LANES:(h + 1) * LANES] = value
            most = jnp.maximum(most, value)
        top[col] = most
    for c in range(blocks):
        top[c] = jnp.broadcast_to(jnp.max(top[c], axis=1, keepdims=True), top.shape[1:])
    for t in range(slots):
        col = cols_ref[t]
        most = top[col]
        part = total[col]
        for value in halves(values_ref, t):
            part = part + jnp.exp2(value - most)
        total[col] = part
    each = LANES // top.shape[1]
    lane = lax.broadcasted_iota(jnp.int32, (LANES, LANES), 1)
    tops = jnp.zeros((LANES, LANES), F32)
    sums = jnp.ones((LANES, LANES), F32)
    for j in range(blocks // each):
        column = range(each * j, each * j + each)
        tops = jnp.where(lane == j, jnp.concatenate([top[c] for c in column], axis=0), tops)
        sums = jnp.where(
            lane == j,
            jnp.concatenate([jnp.sum(total[c], axis=1, keepdims=True) for c in column], axis=0),
            sums,
        )
    rows = blocks // each
    out_ref[...] = tops.T[:rows] + jnp.log2(jnp.maximum(sums.T[:rows], 1.0))


def both_cores(parts_ref, out_ref):
    copies(out_ref, log_sum(parts_ref[...]))


def second_samples(cols_hbm, values_ref, counts_ref, parts_ref, out_ref, weights_ref,
                   cols_ref, sem, bias_cols, slot):
    copy = pltpu.make_async_copy(cols_hbm, cols_ref, sem)
    copy.start()
    slots = values_ref.shape[0]
    expand(log_count(counts_ref) - log_sum(parts_ref[...]), bias_cols, NEG)
    copy.wait()
    for t in range(slots):
        bias = bias_cols[cols_ref[t]]
        for h, value in enumerate(halves(values_ref, t)):
            part = jnp.exp2(bias + value)
            weights_ref[t, :, h * LANES:(h + 1) * LANES] = part
            slot[h * slots + t:h * slots + t + 1] = jnp.maximum(
                jnp.sum(part, axis=0, keepdims=True), jnp.max(part, axis=0, keepdims=True)
            )
    copies(out_ref, slot[...])


def second_states(rows_hbm, cols_hbm, weights_ref, hot_ref, parts_ref, basis_ref, out_ref,
                  rows_ref, cols_ref, sems, scale, sums):
    index = [
        pltpu.make_async_copy(rows_hbm, rows_ref, sems.at[0]), pltpu.make_async_copy(cols_hbm, cols_ref, sems.at[1])
    ]
    for copy in index:
        copy.start()
    blocks = sums.shape[0] - 1
    slots = weights_ref.shape[0]
    count = basis_ref.shape[0]
    width = weights_ref.shape[2]
    cut = width // LANES
    blocks_samp = scale.shape[0] // cut
    parts = jnp.concatenate([by_half(parts_ref, h, slots) for h in range(cut)], axis=1)
    whole = 1.0 / jnp.maximum(row_sums(hot_ref[...], parts), TINY)
    for h in range(cut):
        scale[h * blocks_samp:(h + 1) * blocks_samp] = whole[:, h * LANES:(h + 1) * LANES]
    sums[...] = jnp.zeros(sums.shape, F32)
    ones = jnp.ones((sums.shape[1] - count, width), BF16)
    for copy in index:
        copy.wait()
    for t in range(slots):
        row, col = rows_ref[t], cols_ref[t]
        weight = jnp.concatenate(
            [part * scale[pl.ds(h * blocks_samp + row, 1)] for h, part in enumerate(halves(weights_ref, t))], axis=1
        )
        high = weight.astype(BF16)
        low = (weight - high.astype(F32)).astype(BF16)
        factor = jnp.concatenate([basis_ref[:, pl.ds(pl.multiple_of(row * width, width), width)], ones], axis=0)
        dims = (((1,), (1,)), ((), ()))
        sums[col] += lax.dot_general(factor, high, dims, preferred_element_type=F32) + lax.dot_general(
            factor, low, dims, preferred_element_type=F32
        )
    each = LANES // sums.shape[2]
    across = blocks // each
    half = out_ref.shape[1] // 9
    for j in range(across):
        wide = jnp.concatenate([sums[c] for c in range(each * j, each * j + each)], axis=1)
        for g in range(count // 8):
            owner = g * across + j
            start = owner % half * 9
            out_ref[owner // half, start:start + 8] = wide[8 * g:8 * g + 8]
            out_ref[owner // half, start + 8:start + 9] = wide[count:count + 1]


def core_sums(parts_ref, out_ref):
    mine = my_core()
    value = parts_ref[0, mine] + parts_ref[1, mine]
    for i in range(out_ref.shape[0]):
        for r in range(9):
            out_ref[i, r] = value[9 * i + r:9 * i + r + 1]


def finish(parts_ref, out_ref):
    both = jnp.sum(parts_ref[...], axis=0)
    value = jnp.concatenate([both[r] for r in range(8)], axis=0)
    copies(out_ref, value / both[8])


def my_core():
    return lax.axis_index("core")


def spread(parts, axis):
    return lax.all_to_all(parts, axis, 0, 0)


def pair(parts):
    return lax.all_gather(parts, "core")


def call(kernel, out_shape, in_specs, scratch_shapes=(), limit=40 * MIB):
    single = not isinstance(out_shape, tuple)
    return pl.pallas_call(
        kernel,
        out_shape=out_shape,
        in_specs=in_specs,
        out_specs=vmem(1)[0] if single else tuple(vmem(len(out_shape))),
        scratch_shapes=list(scratch_shapes),
        compiler_params=pltpu.CompilerParams(vmem_limit_bytes=limit),
    )


def on_device(n_core, n_z, n_state, energies, tile_rows, tile_cols, start_free, temps, betas, counts, basis):
    slots, state_block, sample_block = energies.shape
    state_dev = start_free.shape[0]
    blocks = state_dev // state_block
    blocks_samp = basis.shape[1] // sample_block
    cut = sample_block // LANES
    rows = state_dev // LANES
    count = basis.shape[0]
    shape = lambda *dims: jax.ShapeDtypeStruct(dims, F32)
    by_state = (blocks + 1, state_block, LANES)
    place = [
        pltpu.SMEM(tile_rows.shape, jnp.int32), pltpu.SMEM(tile_cols.shape, jnp.int32), pltpu.SemaphoreType.DMA((3,))
    ]
    flat = pltpu.VMEM((rows, LANES), F32)
    whole = pltpu.VMEM((rows, LANES), jnp.int32)
    by_slot = pltpu.VMEM((cut * slots, LANES), F32)

    free, temps, counts = (vector.reshape(rows, LANES) for vector in (start_free, temps, counts))

    parts = call(
        first_samples,
        shape(n_state, cut * slots + 8, LANES),
        hbm(7),
        place[:2] + [
            pltpu.SMEM(betas.shape, F32),
            pltpu.VMEM(energies.shape, F32),
            flat, whole, whole, pltpu.VMEM(by_state, F32), pltpu.VMEM(by_state, F32), by_slot, by_slot,
            pltpu.SemaphoreType.DMA((6 + slots // UNROLL,)),
        ],
        FIRST_VMEM,
    )(tile_rows, tile_cols, betas, energies, free, temps, counts)
    parts = spread(parts, "state")
    parts, values, hot = call(
        first_states,
        (
            shape(rows, LANES), shape(*energies.shape),
            jax.ShapeDtypeStruct((blocks_samp, n_state * slots), BF16),
        ),
        anywhere(3) + vmem(3),
        place + [
            pltpu.SMEM(betas.shape, F32), pltpu.VMEM(by_state, F32), pltpu.VMEM((cut * blocks_samp, LANES), F32),
            pltpu.VMEM(by_state, F32), pltpu.VMEM(by_state, F32),
        ],
    )(tile_rows, tile_cols, betas, temps, energies, parts)
    parts = pair(parts)
    parts = call(both_cores, shape(n_z, rows, LANES), vmem(1))(parts)
    parts = spread(parts, "z")
    parts, weights = call(
        second_samples,
        (shape(n_state, cut * slots, LANES), shape(*energies.shape)),
        anywhere(1) + vmem(3),
        [place[1], pltpu.SemaphoreType.DMA, pltpu.VMEM(by_state, F32), by_slot],
    )(tile_cols, values, counts, parts)
    parts = spread(parts, "state")
    parts = call(
        second_states,
        shape(n_core, n_z * 9, LANES),
        anywhere(2) + vmem(4),
        place + [
            pltpu.VMEM((cut * blocks_samp, LANES), F32), pltpu.VMEM((blocks + 1, count + 16, state_block), F32)
        ],
    )(tile_rows, tile_cols, weights, hot, parts, basis)
    parts = pair(parts)
    parts = call(core_sums, shape(n_z, 9, 1, LANES), vmem(1))(parts)
    parts = spread(parts, "z")
    parts = call(finish, shape(n_z, 8, LANES), vmem(1))(parts)
    parts = spread(parts, "z")
    parts = pair(parts)
    return parts.reshape(count // 8, rows, 8, LANES).transpose(0, 2, 1, 3).reshape(count, state_dev)


def solution(mesh):
    n_samp, n_state = mesh.shape["samp"], mesh.shape["state"]
    n_core = 2
    n_z = n_samp // n_core
    cut = Mesh(mesh.devices.reshape(n_z, n_core, n_state), ("z", "core", "state"))
    samp = ("z", "core")

    def run(*args):
        return on_device(n_core, n_z, n_state, *args)

    return jax.shard_map(
        run,
        mesh=cut,
        in_specs=(
            P(("z", "core", "state"), None, None),
            P(("z", "core", "state")),
            P(("z", "core", "state")),
            P("state"),
            P("state"),
            P(),
            P("state"),
            P(None, samp),
        ),
        out_specs=P(None, "state"),
        check_vma=False,
    )
```

```python
import jax
import jax.numpy as jnp
from jax import lax
from jax.experimental import pallas as pl
from jax.experimental.pallas import tpu as pltpu
from jax.sharding import Mesh, PartitionSpec as P

NEG = -1e30
TINY = 1e-30
LANES = 128
UNROLL = 4
MIB = 1024 * 1024
FIRST_VMEM = 60 * MIB
F32 = jnp.float32
BF16 = jnp.bfloat16
LOG2E = 1.4426950408889634
STEP = 96.0
BASE = -400.0
LAST = 11.0
BITS = 10.0


def vmem(count):
    return [pl.BlockSpec(memory_space=pltpu.VMEM)] * count


def smem(count):
    return [pl.BlockSpec(memory_space=pltpu.SMEM)] * count


def hbm(count):
    return [pl.BlockSpec(memory_space=pltpu.HBM)] * count


def anywhere(count):
    return [pl.BlockSpec(memory_space=pl.ANY)] * count


def state_beta(temps, betas_ref):
    beta = jnp.zeros(temps.shape, F32)
    for i in range(betas_ref.shape[-1]):
        beta = jnp.where(temps == i, betas_ref[:, i:i + 1] if len(betas_ref.shape) == 2 else betas_ref[i], beta)
    return -LOG2E * beta


def log_count(counts_ref):
    return LOG2E * jnp.log(counts_ref[...].astype(F32))


def expand(rows, cols_ref, spare):
    turned = rows.T
    size = cols_ref.shape[1]
    each = LANES // size
    for j in range(rows.shape[0]):
        wide = jnp.broadcast_to(turned[:, j:j + 1], (LANES, LANES))
        for i in range(each):
            cols_ref[each * j + i] = wide[i * size:(i + 1) * size]
    cols_ref[cols_ref.shape[0] - 1] = jnp.full(cols_ref.shape[1:], spare, F32)


def halves(energies_ref, t):
    count = energies_ref.shape[2] // LANES
    return [energies_ref[t, :, h * LANES:(h + 1) * LANES] for h in range(count)]


def copies(out_ref, value):
    for i in range(out_ref.shape[0]):
        out_ref[i] = value


def log_sum(parts):
    top = jnp.max(parts, axis=0)
    return top + jnp.log2(jnp.sum(jnp.exp2(parts - top[None]), axis=0))


def row_sums(hot, values):
    total = None
    for _ in range(3):
        part = values.astype(BF16)
        values = values - part.astype(F32)
        product = jnp.dot(hot, part, preferred_element_type=F32)
        total = product if total is None else total + product
    return total


def by_half(parts_ref, half, slots):
    values = parts_ref[:, half * slots:(half + 1) * slots]
    return values.reshape(values.shape[0] * slots, LANES)


def first_samples(rows_hbm, cols_hbm, betas_hbm, energies_hbm, free_hbm, temps_hbm, counts_hbm,
                  out_ref,
                  rows_ref, cols_ref, betas_ref, energies_ref, free_ref, temps_ref, counts_ref,
                  beta_cols, bias_cols, slot, total, sems):
    slots = energies_ref.shape[0]
    cut = energies_ref.shape[2] // LANES
    small = [
        pltpu.make_async_copy(source, target, sems.at[i])
        for i, (source, target) in enumerate([
            (temps_hbm, temps_ref), (counts_hbm, counts_ref), (free_hbm, free_ref),
            (betas_hbm, betas_ref), (cols_hbm, cols_ref), (rows_hbm, rows_ref),
        ])
    ]
    large = [
        pltpu.make_async_copy(
            energies_hbm.at[pl.ds(g * UNROLL, UNROLL)], energies_ref.at[pl.ds(g * UNROLL, UNROLL)],
            sems.at[len(small) + g],
        )
        for g in range(slots // UNROLL)
    ]
    for copy in small + large:
        copy.start()
    for copy in small:
        copy.wait()
    expand(state_beta(temps_ref[...], betas_ref), beta_cols, 0.0)
    expand(log_count(counts_ref) + LOG2E * free_ref[...], bias_cols, NEG)
    lane = lax.broadcasted_iota(jnp.int32, (1, LANES), 1)
    places = jnp.zeros((1, LANES), F32)
    for t in range(slots):
        places = jnp.where(lane == t, rows_ref[t].astype(F32), places)
    for g in range(slots // UNROLL):
        large[g].wait()
        for t in range(g * UNROLL, (g + 1) * UNROLL):
            beta, bias = beta_cols[cols_ref[t]], bias_cols[cols_ref[t]]
            for h, energy in enumerate(halves(energies_ref, t)):
                score = bias + beta * energy
                peak = jnp.max(score, axis=0, keepdims=True)
                slot[h * slots + t:h * slots + t + 1] = peak
                total[h * slots + t:h * slots + t + 1] = jnp.sum(jnp.exp2(score - peak), axis=0, keepdims=True)
    whole = slot[...] + jnp.log2(jnp.maximum(total[...], 1.0))
    for i in range(out_ref.shape[0]):
        out_ref[i, :cut * slots] = whole
        out_ref[i, cut * slots:] = jnp.broadcast_to(places, (8, LANES))


def first_states(rows_ref, cols_ref, betas_ref, temps_ref, energies_ref, parts_ref, out_ref, values_ref, hot_ref,
                 beta_cols, drop, top, total):
    rows, cols = rows_ref[...], cols_ref[...]
    rows = [rows[0, t] for t in range(energies_ref.shape[0])]
    cols = [cols[0, t] for t in range(energies_ref.shape[0])]
    blocks = beta_cols.shape[0] - 1
    slots = energies_ref.shape[0]
    cut = energies_ref.shape[2] // LANES
    blocks_samp = drop.shape[0] // cut
    wide = []
    for j in range(parts_ref.shape[0] * slots // LANES):
        places = jnp.zeros((1, LANES), F32)
        for i in range(LANES // slots):
            place = parts_ref[j * (LANES // slots) + i, cut * slots:cut * slots + 1]
            place = jnp.where(lax.broadcasted_iota(jnp.int32, place.shape, 1) < slots, place, 0.0)
            places = places + (pltpu.roll(place, i * slots, 1) if i else place)
        wide.append(places)
    wide = jnp.concatenate(wide, axis=1)
    row = lax.broadcasted_iota(jnp.int32, (blocks_samp, wide.shape[1]), 0).astype(F32)
    hot = jnp.where(row == wide, 1.0, 0.0).astype(BF16)
    hot_ref[...] = hot
    parts = jnp.concatenate([by_half(parts_ref, h, slots) for h in range(cut)], axis=1)
    step = jnp.clip(jnp.floor((parts - BASE) * (1.0 / STEP)), 0.0, LAST)
    power = jnp.exp2(BITS * step).astype(BF16)
    found = jnp.maximum(jnp.dot(hot, power, preferred_element_type=F32), 1.0)
    step = jnp.floor(jnp.log2(found) * (1.0 / BITS) + 0.03)
    back = lax.dot_general(hot, step.astype(BF16), (((0,), (0,)), ((), ())), preferred_element_type=F32)
    whole = row_sums(hot, jnp.exp2(parts - (BASE + STEP * back)))
    whole = BASE + STEP * step + jnp.log2(jnp.maximum(whole, 0.5))
    for h in range(cut):
        drop[h * blocks_samp:(h + 1) * blocks_samp] = whole[:, h * LANES:(h + 1) * LANES]
    top[...] = jnp.full(top.shape, NEG, F32)
    total[...] = jnp.zeros(total.shape, F32)
    expand(state_beta(temps_ref[...], betas_ref), beta_cols, 0.0)

    for t in range(slots):
        row, col = rows[t], cols[t]
        beta = beta_cols[col]
        most = top[col]
        for h, energy in enumerate(halves(energies_ref, t)):
            value = beta * energy - drop[pl.ds(h * blocks_samp + row, 1)]
            values_ref[t, :, h * LANES:(h + 1) * LANES] = value
            most = jnp.maximum(most, value)
        top[col] = most
    for t in range(slots):
        col = cols[t]
        most = top[col]
        part = total[col]
        for value in halves(values_ref, t):
            part = part + jnp.exp2(value - most)
        total[col] = part
    each = LANES // top.shape[1]
    for j in range(blocks // each):
        column = range(each * j, each * j + each)
        tops = jnp.concatenate([top[c] for c in column], axis=0).T
        sums = jnp.concatenate([total[c] for c in column], axis=0).T
        peak = jnp.max(tops, axis=0, keepdims=True)
        whole = jnp.sum(sums * jnp.exp2(tops - peak), axis=0, keepdims=True)
        out_ref[j:j + 1] = peak + jnp.log2(jnp.maximum(whole, 1.0))


def both_cores(parts_ref, out_ref):
    copies(out_ref, log_sum(parts_ref[...]))


def second_samples(cols_ref, values_ref, counts_ref, parts_ref, out_ref, weights_ref,
                   bias_cols, slot):
    cols = cols_ref[...]
    cols = [cols[0, t] for t in range(values_ref.shape[0])]
    slots = values_ref.shape[0]
    expand(log_count(counts_ref) - log_sum(parts_ref[...]), bias_cols, NEG)
    for t in range(slots):
        bias = bias_cols[cols[t]]
        for h, value in enumerate(halves(values_ref, t)):
            part = jnp.exp2(bias + value)
            weights_ref[t, :, h * LANES:(h + 1) * LANES] = part
            slot[h * slots + t:h * slots + t + 1] = jnp.maximum(
                jnp.sum(part, axis=0, keepdims=True), jnp.max(part, axis=0, keepdims=True)
            )
    copies(out_ref, slot[...])


def second_states(rows_ref, cols_ref, weights_ref, hot_ref, parts_ref, basis_ref, out_ref, scale, sums):
    rows, cols = rows_ref[...], cols_ref[...]
    rows = [rows[0, t] for t in range(weights_ref.shape[0])]
    cols = [cols[0, t] for t in range(weights_ref.shape[0])]
    blocks = sums.shape[0] - 1
    slots = weights_ref.shape[0]
    count = basis_ref.shape[0]
    width = weights_ref.shape[2]
    cut = width // LANES
    blocks_samp = scale.shape[0] // cut
    parts = jnp.concatenate([by_half(parts_ref, h, slots) for h in range(cut)], axis=1)
    whole = 1.0 / jnp.maximum(row_sums(hot_ref[...], parts), TINY)
    for h in range(cut):
        scale[h * blocks_samp:(h + 1) * blocks_samp] = whole[:, h * LANES:(h + 1) * LANES]
    sums[...] = jnp.zeros(sums.shape, F32)
    ones = jnp.ones((sums.shape[1] - count, width), BF16)
    for t in range(slots):
        row, col = rows[t], cols[t]
        weight = jnp.concatenate(
            [part * scale[pl.ds(h * blocks_samp + row, 1)] for h, part in enumerate(halves(weights_ref, t))], axis=1
        )
        high = weight.astype(BF16)
        low = (weight - high.astype(F32)).astype(BF16)
        factor = jnp.concatenate([basis_ref[:, pl.ds(pl.multiple_of(row * width, width), width)], ones], axis=0)
        dims = (((1,), (1,)), ((), ()))
        sums[col] += lax.dot_general(factor, high, dims, preferred_element_type=F32) + lax.dot_general(
            factor, low, dims, preferred_element_type=F32
        )
    each = LANES // sums.shape[2]
    across = blocks // each
    half = out_ref.shape[1] // 9
    for j in range(across):
        wide = jnp.concatenate([sums[c] for c in range(each * j, each * j + each)], axis=1)
        for g in range(count // 8):
            owner = g * across + j
            start = owner % half * 9
            out_ref[owner // half, start:start + 8] = wide[8 * g:8 * g + 8]
            out_ref[owner // half, start + 8:start + 9] = wide[count:count + 1]


def core_sums(parts_ref, out_ref):
    mine = my_core()
    value = parts_ref[0, mine] + parts_ref[1, mine]
    for i in range(out_ref.shape[0]):
        for r in range(9):
            out_ref[i, r] = value[9 * i + r:9 * i + r + 1]


def finish(parts_ref, out_ref):
    both = jnp.sum(parts_ref[...], axis=0)
    value = jnp.concatenate([both[r] for r in range(8)], axis=0)
    copies(out_ref, value / both[8])


def my_core():
    return lax.axis_index("core")


def spread(parts, axis):
    return lax.all_to_all(parts, axis, 0, 0)


def pair(parts):
    return lax.all_gather(parts, "core")


def call(kernel, out_shape, in_specs, scratch_shapes=(), limit=40 * MIB):
    single = not isinstance(out_shape, tuple)
    return pl.pallas_call(
        kernel,
        out_shape=out_shape,
        in_specs=in_specs,
        out_specs=vmem(1)[0] if single else tuple(vmem(len(out_shape))),
        scratch_shapes=list(scratch_shapes),
        compiler_params=pltpu.CompilerParams(vmem_limit_bytes=limit),
    )


def on_device(n_core, n_z, n_state, energies, tile_rows, tile_cols, start_free, temps, betas, counts, basis):
    slots, state_block, sample_block = energies.shape
    state_dev = start_free.shape[0]
    blocks = state_dev // state_block
    blocks_samp = basis.shape[1] // sample_block
    cut = sample_block // LANES
    rows = state_dev // LANES
    count = basis.shape[0]
    shape = lambda *dims: jax.ShapeDtypeStruct(dims, F32)
    by_state = (blocks + 1, state_block, LANES)
    place = [
        pltpu.SMEM(tile_rows.shape, jnp.int32), pltpu.SMEM(tile_cols.shape, jnp.int32), pltpu.SemaphoreType.DMA((3,))
    ]
    flat = pltpu.VMEM((rows, LANES), F32)
    whole = pltpu.VMEM((rows, LANES), jnp.int32)
    by_slot = pltpu.VMEM((cut * slots, LANES), F32)

    free, temps, counts = (vector.reshape(rows, LANES) for vector in (start_free, temps, counts))

    parts = call(
        first_samples,
        shape(n_state, cut * slots + 8, LANES),
        hbm(7),
        place[:2] + [
            pltpu.SMEM(betas.shape, F32),
            pltpu.VMEM(energies.shape, F32),
            flat, whole, whole, pltpu.VMEM(by_state, F32), pltpu.VMEM(by_state, F32), by_slot, by_slot,
            pltpu.SemaphoreType.DMA((6 + slots // UNROLL,)),
        ],
        FIRST_VMEM,
    )(tile_rows, tile_cols, betas, energies, free, temps, counts)
    parts = spread(parts, "state")
    parts, values, hot = call(
        first_states,
        (
            shape(rows, LANES), shape(*energies.shape),
            jax.ShapeDtypeStruct((blocks_samp, n_state * slots), BF16),
        ),
        vmem(6),
        [
            pltpu.VMEM(by_state, F32), pltpu.VMEM((cut * blocks_samp, LANES), F32),
            pltpu.VMEM(by_state, F32), pltpu.VMEM(by_state, F32),
        ],
    )(tile_rows.reshape(1, slots), tile_cols.reshape(1, slots), betas.reshape(1, -1), temps, energies, parts)
    parts = pair(parts)
    parts = call(both_cores, shape(n_z, rows, LANES), vmem(1))(parts)
    parts = spread(parts, "z")
    parts, weights = call(
        second_samples,
        (shape(n_state, cut * slots, LANES), shape(*energies.shape)),
        vmem(4),
        [pltpu.VMEM(by_state, F32), by_slot],
    )(tile_cols.reshape(1, slots), values, counts, parts)
    parts = spread(parts, "state")
    parts = call(
        second_states,
        shape(n_core, n_z * 9, LANES),
        vmem(6),
        [
            pltpu.VMEM((cut * blocks_samp, LANES), F32), pltpu.VMEM((blocks + 1, count + 16, state_block), F32)
        ],
    )(tile_rows.reshape(1, slots), tile_cols.reshape(1, slots), weights, hot, parts, basis)
    parts = pair(parts)
    parts = call(core_sums, shape(n_z, 9, 1, LANES), vmem(1))(parts)
    parts = spread(parts, "z")
    parts = call(finish, shape(n_z, 8, LANES), vmem(1))(parts)
    parts = spread(parts, "z")
    parts = pair(parts)
    return parts.reshape(count // 8, rows, 8, LANES).transpose(0, 2, 1, 3).reshape(count, state_dev)


def solution(mesh):
    n_samp, n_state = mesh.shape["samp"], mesh.shape["state"]
    n_core = 2
    n_z = n_samp // n_core
    cut = Mesh(mesh.devices.reshape(n_z, n_core, n_state), ("z", "core", "state"))
    samp = ("z", "core")

    def run(*args):
        return on_device(n_core, n_z, n_state, *args)

    return jax.shard_map(
        run,
        mesh=cut,
        in_specs=(
            P(("z", "core", "state"), None, None),
            P(("z", "core", "state")),
            P(("z", "core", "state")),
            P("state"),
            P("state"),
            P(),
            P("state"),
            P(None, samp),
        ),
        out_specs=P(None, "state"),
        check_vma=False,
    )
```

```python
import jax
import jax.numpy as jnp
from jax import lax
from jax.experimental import pallas as pl
from jax.experimental.pallas import tpu as pltpu
from jax.sharding import Mesh, PartitionSpec as P

NEG = -1e30
TINY = 1e-30
LANES = 128
UNROLL = 4
MIB = 1024 * 1024
FIRST_VMEM = 60 * MIB
F32 = jnp.float32
BF16 = jnp.bfloat16
LOG2E = 1.4426950408889634
STEP = 96.0
BASE = -400.0
LAST = 11.0
BITS = 10.0


def vmem(count):
    return [pl.BlockSpec(memory_space=pltpu.VMEM)] * count


def smem(count):
    return [pl.BlockSpec(memory_space=pltpu.SMEM)] * count


def hbm(count):
    return [pl.BlockSpec(memory_space=pltpu.HBM)] * count


def anywhere(count):
    return [pl.BlockSpec(memory_space=pl.ANY)] * count


def state_beta(temps, betas_ref):
    beta = jnp.zeros(temps.shape, F32)
    for i in range(betas_ref.shape[-1]):
        beta = jnp.where(temps == i, betas_ref[:, i:i + 1] if len(betas_ref.shape) == 2 else betas_ref[i], beta)
    return -LOG2E * beta


def log_count(counts_ref):
    return LOG2E * jnp.log(counts_ref[...].astype(F32))


def expand(rows, cols_ref, spare):
    turned = rows.T
    size = cols_ref.shape[1]
    each = LANES // size
    for j in range(rows.shape[0]):
        wide = jnp.broadcast_to(turned[:, j:j + 1], (LANES, LANES))
        for i in range(each):
            cols_ref[each * j + i] = wide[i * size:(i + 1) * size]
    cols_ref[cols_ref.shape[0] - 1] = jnp.full(cols_ref.shape[1:], spare, F32)


def halves(energies_ref, t):
    count = energies_ref.shape[2] // LANES
    return [energies_ref[t, :, h * LANES:(h + 1) * LANES] for h in range(count)]


def copies(out_ref, value):
    for i in range(out_ref.shape[0]):
        out_ref[i] = value


def log_sum(parts):
    top = jnp.max(parts, axis=0)
    return top + jnp.log2(jnp.sum(jnp.exp2(parts - top[None]), axis=0))


def row_sums(hot, values):
    total = None
    for _ in range(3):
        part = values.astype(BF16)
        values = values - part.astype(F32)
        product = jnp.dot(hot, part, preferred_element_type=F32)
        total = product if total is None else total + product
    return total


def by_half(parts_ref, half, slots):
    values = parts_ref[:, half * slots:(half + 1) * slots]
    return values.reshape(values.shape[0] * slots, LANES)


def first_samples(rows_hbm, cols_hbm, betas_hbm, energies_hbm, free_hbm, temps_hbm, counts_hbm,
                  out_ref,
                  rows_ref, cols_ref, betas_ref, energies_ref, free_ref, temps_ref, counts_ref,
                  beta_cols, bias_cols, slot, total, sems):
    slots = energies_ref.shape[0]
    cut = energies_ref.shape[2] // LANES
    small = [
        pltpu.make_async_copy(source, target, sems.at[i])
        for i, (source, target) in enumerate([
            (temps_hbm, temps_ref), (counts_hbm, counts_ref), (free_hbm, free_ref),
            (betas_hbm, betas_ref), (cols_hbm, cols_ref), (rows_hbm, rows_ref),
        ])
    ]
    large = [
        pltpu.make_async_copy(
            energies_hbm.at[pl.ds(g * UNROLL, UNROLL)], energies_ref.at[pl.ds(g * UNROLL, UNROLL)],
            sems.at[len(small) + g],
        )
        for g in range(slots // UNROLL)
    ]
    for copy in small + large:
        copy.start()
    for copy in small:
        copy.wait()
    expand(state_beta(temps_ref[...], betas_ref), beta_cols, 0.0)
    expand(log_count(counts_ref) + LOG2E * free_ref[...], bias_cols, NEG)
    lane = lax.broadcasted_iota(jnp.int32, (1, LANES), 1)
    places = jnp.zeros((1, LANES), F32)
    for t in range(slots):
        places = jnp.where(lane == t, rows_ref[t].astype(F32), places)
    for g in range(slots // UNROLL):
        large[g].wait()
        for t in range(g * UNROLL, (g + 1) * UNROLL):
            beta, bias = beta_cols[cols_ref[t]], bias_cols[cols_ref[t]]
            for h, energy in enumerate(halves(energies_ref, t)):
                score = bias + beta * energy
                peak = jnp.max(score, axis=0, keepdims=True)
                slot[h * slots + t:h * slots + t + 1] = peak
                total[h * slots + t:h * slots + t + 1] = jnp.sum(jnp.exp2(score - peak), axis=0, keepdims=True)
    whole = slot[...] + jnp.log2(jnp.maximum(total[...], 1.0))
    each = cut * slots + 1
    for i in range(out_ref.shape[0] // each):
        out_ref[i * each:(i + 1) * each - 1] = whole
        out_ref[(i + 1) * each - 1:(i + 1) * each] = places


def first_states(rows_ref, cols_ref, betas_ref, temps_ref, energies_ref, parts_ref, out_ref, values_ref, hot_ref,
                 beta_cols, drop, top, total):
    rows, cols = rows_ref[...], cols_ref[...]
    rows = [rows[0, t] for t in range(energies_ref.shape[0])]
    cols = [cols[0, t] for t in range(energies_ref.shape[0])]
    blocks = beta_cols.shape[0] - 1
    slots = energies_ref.shape[0]
    cut = energies_ref.shape[2] // LANES
    blocks_samp = drop.shape[0] // cut
    wide = []
    each = cut * slots + 1
    peers = parts_ref.shape[0] // each
    for j in range(peers * slots // LANES):
        places = jnp.zeros((1, LANES), F32)
        for i in range(LANES // slots):
            end = (j * (LANES // slots) + i + 1) * each
            place = parts_ref[end - 1:end]
            place = jnp.where(lax.broadcasted_iota(jnp.int32, place.shape, 1) < slots, place, 0.0)
            places = places + (pltpu.roll(place, i * slots, 1) if i else place)
        wide.append(places)
    wide = jnp.concatenate(wide, axis=1)
    row = lax.broadcasted_iota(jnp.int32, (blocks_samp, wide.shape[1]), 0).astype(F32)
    hot = jnp.where(row == wide, 1.0, 0.0).astype(BF16)
    hot_ref[...] = hot
    parts = jnp.concatenate(
        [
            jnp.concatenate(
                [parts_ref[i * each + h * slots:i * each + (h + 1) * slots] for i in range(peers)], axis=0
            )
            for h in range(cut)
        ],
        axis=1,
    )
    step = jnp.clip(jnp.floor((parts - BASE) * (1.0 / STEP)), 0.0, LAST)
    power = jnp.exp2(BITS * step).astype(BF16)
    found = jnp.maximum(jnp.dot(hot, power, preferred_element_type=F32), 1.0)
    step = jnp.floor(jnp.log2(found) * (1.0 / BITS) + 0.03)
    back = lax.dot_general(hot, step.astype(BF16), (((0,), (0,)), ((), ())), preferred_element_type=F32)
    whole = row_sums(hot, jnp.exp2(parts - (BASE + STEP * back)))
    whole = BASE + STEP * step + jnp.log2(jnp.maximum(whole, 0.5))
    for h in range(cut):
        drop[h * blocks_samp:(h + 1) * blocks_samp] = whole[:, h * LANES:(h + 1) * LANES]
    top[...] = jnp.full(top.shape, NEG, F32)
    total[...] = jnp.zeros(total.shape, F32)
    expand(state_beta(temps_ref[...], betas_ref), beta_cols, 0.0)

    for t in range(slots):
        row, col = rows[t], cols[t]
        beta = beta_cols[col]
        most = top[col]
        for h, energy in enumerate(halves(energies_ref, t)):
            value = beta * energy - drop[pl.ds(h * blocks_samp + row, 1)]
            values_ref[t, :, h * LANES:(h + 1) * LANES] = value
            most = jnp.maximum(most, value)
        top[col] = most
    for t in range(slots):
        col = cols[t]
        most = top[col]
        part = total[col]
        for value in halves(values_ref, t):
            part = part + jnp.exp2(value - most)
        total[col] = part
    each = LANES // top.shape[1]
    for j in range(blocks // each):
        column = range(each * j, each * j + each)
        tops = jnp.concatenate([top[c] for c in column], axis=0).T
        sums = jnp.concatenate([total[c] for c in column], axis=0).T
        peak = jnp.max(tops, axis=0, keepdims=True)
        whole = jnp.sum(sums * jnp.exp2(tops - peak), axis=0, keepdims=True)
        out_ref[j:j + 1] = peak + jnp.log2(jnp.maximum(whole, 1.0))


def both_cores(parts_ref, out_ref):
    copies(out_ref, log_sum(parts_ref[...]))


def second_samples(cols_ref, values_ref, counts_ref, parts_ref, out_ref, weights_ref,
                   bias_cols, slot):
    cols = cols_ref[...]
    cols = [cols[0, t] for t in range(values_ref.shape[0])]
    slots = values_ref.shape[0]
    expand(log_count(counts_ref) - log_sum(parts_ref[...]), bias_cols, NEG)
    for t in range(slots):
        bias = bias_cols[cols[t]]
        for h, value in enumerate(halves(values_ref, t)):
            part = jnp.exp2(bias + value)
            weights_ref[t, :, h * LANES:(h + 1) * LANES] = part
            slot[h * slots + t:h * slots + t + 1] = jnp.maximum(
                jnp.sum(part, axis=0, keepdims=True), jnp.max(part, axis=0, keepdims=True)
            )
    copies(out_ref, slot[...])


def second_states(rows_ref, cols_ref, weights_ref, hot_ref, parts_ref, basis_ref, out_ref, scale, sums):
    rows, cols = rows_ref[...], cols_ref[...]
    rows = [rows[0, t] for t in range(weights_ref.shape[0])]
    cols = [cols[0, t] for t in range(weights_ref.shape[0])]
    blocks = sums.shape[0] - 1
    slots = weights_ref.shape[0]
    count = basis_ref.shape[0]
    width = weights_ref.shape[2]
    cut = width // LANES
    blocks_samp = scale.shape[0] // cut
    parts = jnp.concatenate([by_half(parts_ref, h, slots) for h in range(cut)], axis=1)
    whole = 1.0 / jnp.maximum(row_sums(hot_ref[...], parts), TINY)
    for h in range(cut):
        scale[h * blocks_samp:(h + 1) * blocks_samp] = whole[:, h * LANES:(h + 1) * LANES]
    sums[...] = jnp.zeros(sums.shape, F32)
    ones = jnp.ones((sums.shape[1] - count, width), BF16)
    for t in range(slots):
        row, col = rows[t], cols[t]
        weight = jnp.concatenate(
            [part * scale[pl.ds(h * blocks_samp + row, 1)] for h, part in enumerate(halves(weights_ref, t))], axis=1
        )
        high = weight.astype(BF16)
        low = (weight - high.astype(F32)).astype(BF16)
        factor = jnp.concatenate([basis_ref[:, pl.ds(pl.multiple_of(row * width, width), width)], ones], axis=0)
        dims = (((1,), (1,)), ((), ()))
        sums[col] += lax.dot_general(factor, high, dims, preferred_element_type=F32) + lax.dot_general(
            factor, low, dims, preferred_element_type=F32
        )
    each = LANES // sums.shape[2]
    across = blocks // each
    half = out_ref.shape[1] // 9
    for j in range(across):
        wide = jnp.concatenate([sums[c] for c in range(each * j, each * j + each)], axis=1)
        for g in range(count // 8):
            owner = g * across + j
            start = owner % half * 9
            out_ref[owner // half, start:start + 8] = wide[8 * g:8 * g + 8]
            out_ref[owner // half, start + 8:start + 9] = wide[count:count + 1]


def core_sums(parts_ref, out_ref):
    mine = my_core()
    value = parts_ref[0, mine] + parts_ref[1, mine]
    for i in range(out_ref.shape[0]):
        for r in range(9):
            out_ref[i, r] = value[9 * i + r:9 * i + r + 1]


def finish(parts_ref, out_ref):
    both = jnp.sum(parts_ref[...], axis=0)
    value = jnp.concatenate([both[r] for r in range(8)], axis=0)
    copies(out_ref, value / both[8])


def my_core():
    return lax.axis_index("core")


def spread(parts, axis):
    return lax.all_to_all(parts, axis, 0, 0)


def pair(parts):
    return lax.all_gather(parts, "core")


def call(kernel, out_shape, in_specs, scratch_shapes=(), limit=40 * MIB):
    single = not isinstance(out_shape, tuple)
    return pl.pallas_call(
        kernel,
        out_shape=out_shape,
        in_specs=in_specs,
        out_specs=vmem(1)[0] if single else tuple(vmem(len(out_shape))),
        scratch_shapes=list(scratch_shapes),
        compiler_params=pltpu.CompilerParams(vmem_limit_bytes=limit),
    )


def on_device(n_core, n_z, n_state, energies, tile_rows, tile_cols, start_free, temps, betas, counts, basis):
    slots, state_block, sample_block = energies.shape
    state_dev = start_free.shape[0]
    blocks = state_dev // state_block
    blocks_samp = basis.shape[1] // sample_block
    cut = sample_block // LANES
    rows = state_dev // LANES
    count = basis.shape[0]
    shape = lambda *dims: jax.ShapeDtypeStruct(dims, F32)
    by_state = (blocks + 1, state_block, LANES)
    place = [
        pltpu.SMEM(tile_rows.shape, jnp.int32), pltpu.SMEM(tile_cols.shape, jnp.int32), pltpu.SemaphoreType.DMA((3,))
    ]
    flat = pltpu.VMEM((rows, LANES), F32)
    whole = pltpu.VMEM((rows, LANES), jnp.int32)
    by_slot = pltpu.VMEM((cut * slots, LANES), F32)

    free, temps, counts = (vector.reshape(rows, LANES) for vector in (start_free, temps, counts))

    parts = call(
        first_samples,
        shape(n_state * (cut * slots + 1), LANES),
        hbm(7),
        place[:2] + [
            pltpu.SMEM(betas.shape, F32),
            pltpu.VMEM(energies.shape, F32),
            flat, whole, whole, pltpu.VMEM(by_state, F32), pltpu.VMEM(by_state, F32), by_slot, by_slot,
            pltpu.SemaphoreType.DMA((6 + slots // UNROLL,)),
        ],
        FIRST_VMEM,
    )(tile_rows, tile_cols, betas, energies, free, temps, counts)
    parts = spread(parts.reshape(n_state, cut * slots + 1, 1, LANES), "state").reshape(-1, LANES)
    parts, values, hot = call(
        first_states,
        (
            shape(rows, LANES), shape(*energies.shape),
            jax.ShapeDtypeStruct((blocks_samp, n_state * slots), BF16),
        ),
        vmem(6),
        [
            pltpu.VMEM(by_state, F32), pltpu.VMEM((cut * blocks_samp, LANES), F32),
            pltpu.VMEM(by_state, F32), pltpu.VMEM(by_state, F32),
        ],
    )(tile_rows.reshape(1, slots), tile_cols.reshape(1, slots), betas.reshape(1, -1), temps, energies, parts)
    parts = pair(parts)
    parts = call(both_cores, shape(n_z, rows, LANES), vmem(1))(parts)
    parts = spread(parts, "z")
    parts, weights = call(
        second_samples,
        (shape(n_state, cut * slots, LANES), shape(*energies.shape)),
        vmem(4),
        [pltpu.VMEM(by_state, F32), by_slot],
    )(tile_cols.reshape(1, slots), values, counts, parts)
    parts = spread(parts, "state")
    parts = call(
        second_states,
        shape(n_core, n_z * 9, LANES),
        vmem(6),
        [
            pltpu.VMEM((cut * blocks_samp, LANES), F32), pltpu.VMEM((blocks + 1, count + 16, state_block), F32)
        ],
    )(tile_rows.reshape(1, slots), tile_cols.reshape(1, slots), weights, hot, parts, basis)
    parts = pair(parts)
    parts = call(core_sums, shape(n_z, 9, 1, LANES), vmem(1))(parts)
    parts = spread(parts, "z")
    parts = call(finish, shape(n_z, 8, LANES), vmem(1))(parts)
    parts = spread(parts, "z")
    parts = pair(parts)
    return parts.reshape(count // 8, rows, 8, LANES).transpose(0, 2, 1, 3).reshape(count, state_dev)


def solution(mesh):
    n_samp, n_state = mesh.shape["samp"], mesh.shape["state"]
    n_core = 2
    n_z = n_samp // n_core
    cut = Mesh(mesh.devices.reshape(n_z, n_core, n_state), ("z", "core", "state"))
    samp = ("z", "core")

    def run(*args):
        return on_device(n_core, n_z, n_state, *args)

    return jax.shard_map(
        run,
        mesh=cut,
        in_specs=(
            P(("z", "core", "state"), None, None),
            P(("z", "core", "state")),
            P(("z", "core", "state")),
            P("state"),
            P("state"),
            P(),
            P("state"),
            P(None, samp),
        ),
        out_specs=P(None, "state"),
        check_vma=False,
    )
```

```python
import jax
import jax.numpy as jnp
from jax import lax
from jax.experimental import pallas as pl
from jax.experimental.pallas import tpu as pltpu
from jax.sharding import Mesh, PartitionSpec as P

NEG = -1e30
TINY = 1e-30
LANES = 128
UNROLL = 8
MIB = 1024 * 1024
FIRST_VMEM = 60 * MIB
F32 = jnp.float32
BF16 = jnp.bfloat16
LOG2E = 1.4426950408889634
STEP = 96.0
BASE = -400.0
LAST = 11.0
BITS = 10.0


def vmem(count):
    return [pl.BlockSpec(memory_space=pltpu.VMEM)] * count


def smem(count):
    return [pl.BlockSpec(memory_space=pltpu.SMEM)] * count


def hbm(count):
    return [pl.BlockSpec(memory_space=pltpu.HBM)] * count


def anywhere(count):
    return [pl.BlockSpec(memory_space=pl.ANY)] * count


def state_beta(temps, betas_ref):
    beta = jnp.zeros(temps.shape, F32)
    for i in range(betas_ref.shape[-1]):
        beta = jnp.where(temps == i, betas_ref[:, i:i + 1] if len(betas_ref.shape) == 2 else betas_ref[i], beta)
    return -LOG2E * beta


def log_count(counts_ref):
    return LOG2E * jnp.log(counts_ref[...].astype(F32))


def expand(rows, cols_ref, spare):
    turned = rows.T
    size = cols_ref.shape[1]
    each = LANES // size
    for j in range(rows.shape[0]):
        wide = jnp.broadcast_to(turned[:, j:j + 1], (LANES, LANES))
        for i in range(each):
            cols_ref[each * j + i] = wide[i * size:(i + 1) * size]
    cols_ref[cols_ref.shape[0] - 1] = jnp.full(cols_ref.shape[1:], spare, F32)


def halves(energies_ref, t):
    count = energies_ref.shape[2] // LANES
    return [energies_ref[t, :, h * LANES:(h + 1) * LANES] for h in range(count)]


def copies(out_ref, value):
    for i in range(out_ref.shape[0]):
        out_ref[i] = value


def log_sum(parts):
    top = jnp.max(parts, axis=0)
    return top + jnp.log2(jnp.sum(jnp.exp2(parts - top[None]), axis=0))


def row_sums(hot, values):
    total = None
    for _ in range(3):
        part = values.astype(BF16)
        values = values - part.astype(F32)
        product = jnp.dot(hot, part, preferred_element_type=F32)
        total = product if total is None else total + product
    return total


def by_half(parts_ref, half, slots):
    values = parts_ref[:, half * slots:(half + 1) * slots]
    return values.reshape(values.shape[0] * slots, LANES)


def first_samples(rows_hbm, cols_hbm, betas_hbm, energies_hbm, free_hbm, temps_hbm, counts_hbm,
                  out_ref,
                  rows_ref, cols_ref, betas_ref, energies_ref, free_ref, temps_ref, counts_ref,
                  beta_cols, bias_cols, slot, total, sems):
    slots = energies_ref.shape[0]
    cut = energies_ref.shape[2] // LANES
    small = [
        pltpu.make_async_copy(source, target, sems.at[i])
        for i, (source, target) in enumerate([
            (temps_hbm, temps_ref), (counts_hbm, counts_ref), (free_hbm, free_ref),
            (betas_hbm, betas_ref), (cols_hbm, cols_ref), (rows_hbm, rows_ref),
        ])
    ]
    large = [
        pltpu.make_async_copy(
            energies_hbm.at[pl.ds(g * UNROLL, UNROLL)], energies_ref.at[pl.ds(g * UNROLL, UNROLL)],
            sems.at[len(small) + g],
        )
        for g in range(slots // UNROLL)
    ]
    for copy in small + large:
        copy.start()
    for copy in small:
        copy.wait()
    expand(state_beta(temps_ref[...], betas_ref), beta_cols, 0.0)
    expand(log_count(counts_ref) + LOG2E * free_ref[...], bias_cols, NEG)
    lane = lax.broadcasted_iota(jnp.int32, (1, LANES), 1)
    places = jnp.zeros((1, LANES), F32)
    for t in range(slots):
        places = jnp.where(lane == t, rows_ref[t].astype(F32), places)
    for g in range(slots // UNROLL):
        large[g].wait()
        for t in range(g * UNROLL, (g + 1) * UNROLL):
            beta, bias = beta_cols[cols_ref[t]], bias_cols[cols_ref[t]]
            for h, energy in enumerate(halves(energies_ref, t)):
                score = bias + beta * energy
                peak = jnp.max(score, axis=0, keepdims=True)
                slot[h * slots + t:h * slots + t + 1] = peak
                total[h * slots + t:h * slots + t + 1] = jnp.sum(jnp.exp2(score - peak), axis=0, keepdims=True)
    whole = slot[...] + jnp.log2(jnp.maximum(total[...], 1.0))
    each = cut * slots + 1
    for i in range(out_ref.shape[0] // each):
        out_ref[i * each:(i + 1) * each - 1] = whole
        out_ref[(i + 1) * each - 1:(i + 1) * each] = places


def first_states(rows_ref, cols_ref, betas_ref, temps_ref, energies_ref, parts_ref, out_ref, values_ref, hot_ref,
                 beta_cols, drop, top, total):
    rows, cols = rows_ref[...], cols_ref[...]
    rows = [rows[0, t] for t in range(energies_ref.shape[0])]
    cols = [cols[0, t] for t in range(energies_ref.shape[0])]
    blocks = beta_cols.shape[0] - 1
    slots = energies_ref.shape[0]
    cut = energies_ref.shape[2] // LANES
    blocks_samp = drop.shape[0] // cut
    wide = []
    each = cut * slots + 1
    peers = parts_ref.shape[0] // each
    for j in range(peers * slots // LANES):
        places = jnp.zeros((1, LANES), F32)
        for i in range(LANES // slots):
            end = (j * (LANES // slots) + i + 1) * each
            place = parts_ref[end - 1:end]
            place = jnp.where(lax.broadcasted_iota(jnp.int32, place.shape, 1) < slots, place, 0.0)
            places = places + (pltpu.roll(place, i * slots, 1) if i else place)
        wide.append(places)
    wide = jnp.concatenate(wide, axis=1)
    row = lax.broadcasted_iota(jnp.int32, (blocks_samp, wide.shape[1]), 0).astype(F32)
    hot = jnp.where(row == wide, 1.0, 0.0).astype(BF16)
    hot_ref[...] = hot
    parts = jnp.concatenate(
        [
            jnp.concatenate(
                [parts_ref[i * each + h * slots:i * each + (h + 1) * slots] for i in range(peers)], axis=0
            )
            for h in range(cut)
        ],
        axis=1,
    )
    step = jnp.clip(jnp.floor((parts - BASE) * (1.0 / STEP)), 0.0, LAST)
    power = jnp.exp2(BITS * step).astype(BF16)
    found = jnp.maximum(jnp.dot(hot, power, preferred_element_type=F32), 1.0)
    step = jnp.floor(jnp.log2(found) * (1.0 / BITS) + 0.03)
    back = lax.dot_general(hot, step.astype(BF16), (((0,), (0,)), ((), ())), preferred_element_type=F32)
    whole = row_sums(hot, jnp.exp2(parts - (BASE + STEP * back)))
    whole = BASE + STEP * step + jnp.log2(jnp.maximum(whole, 0.5))
    for h in range(cut):
        drop[h * blocks_samp:(h + 1) * blocks_samp] = whole[:, h * LANES:(h + 1) * LANES]
    top[...] = jnp.full(top.shape, NEG, F32)
    total[...] = jnp.zeros(total.shape, F32)
    expand(state_beta(temps_ref[...], betas_ref), beta_cols, 0.0)

    for t in range(slots):
        row, col = rows[t], cols[t]
        beta = beta_cols[col]
        most = top[col]
        for h, energy in enumerate(halves(energies_ref, t)):
            value = beta * energy - drop[pl.ds(h * blocks_samp + row, 1)]
            values_ref[t, :, h * LANES:(h + 1) * LANES] = value
            most = jnp.maximum(most, value)
        top[col] = most
    for t in range(slots):
        col = cols[t]
        most = top[col]
        part = total[col]
        for value in halves(values_ref, t):
            part = part + jnp.exp2(value - most)
        total[col] = part
    each = LANES // top.shape[1]
    for j in range(blocks // each):
        column = range(each * j, each * j + each)
        tops = jnp.concatenate([top[c] for c in column], axis=0).T
        sums = jnp.concatenate([total[c] for c in column], axis=0).T
        peak = jnp.max(tops, axis=0, keepdims=True)
        whole = jnp.sum(sums * jnp.exp2(tops - peak), axis=0, keepdims=True)
        out_ref[j:j + 1] = peak + jnp.log2(jnp.maximum(whole, 1.0))


def both_cores(parts_ref, out_ref):
    copies(out_ref, log_sum(parts_ref[...]))


def second_samples(cols_ref, values_ref, counts_ref, parts_ref, out_ref, weights_ref,
                   bias_cols, slot):
    cols = cols_ref[...]
    cols = [cols[0, t] for t in range(values_ref.shape[0])]
    slots = values_ref.shape[0]
    expand(log_count(counts_ref) - log_sum(parts_ref[...]), bias_cols, NEG)
    for t in range(slots):
        bias = bias_cols[cols[t]]
        for h, value in enumerate(halves(values_ref, t)):
            part = jnp.exp2(bias + value)
            weights_ref[t, :, h * LANES:(h + 1) * LANES] = part
            slot[h * slots + t:h * slots + t + 1] = jnp.maximum(
                jnp.sum(part, axis=0, keepdims=True), jnp.max(part, axis=0, keepdims=True)
            )
    copies(out_ref, slot[...])


def second_states(rows_ref, cols_ref, weights_ref, hot_ref, parts_ref, basis_ref, out_ref, scale, sums):
    rows, cols = rows_ref[...], cols_ref[...]
    rows = [rows[0, t] for t in range(weights_ref.shape[0])]
    cols = [cols[0, t] for t in range(weights_ref.shape[0])]
    blocks = sums.shape[0] - 1
    slots = weights_ref.shape[0]
    count = basis_ref.shape[0]
    width = weights_ref.shape[2]
    cut = width // LANES
    blocks_samp = scale.shape[0] // cut
    parts = jnp.concatenate([by_half(parts_ref, h, slots) for h in range(cut)], axis=1)
    whole = 1.0 / jnp.maximum(row_sums(hot_ref[...], parts), TINY)
    for h in range(cut):
        scale[h * blocks_samp:(h + 1) * blocks_samp] = whole[:, h * LANES:(h + 1) * LANES]
    sums[...] = jnp.zeros(sums.shape, F32)
    ones = jnp.ones((sums.shape[1] - count, width), BF16)
    for t in range(slots):
        row, col = rows[t], cols[t]
        weight = jnp.concatenate(
            [part * scale[pl.ds(h * blocks_samp + row, 1)] for h, part in enumerate(halves(weights_ref, t))], axis=1
        )
        high = weight.astype(BF16)
        low = (weight - high.astype(F32)).astype(BF16)
        factor = jnp.concatenate([basis_ref[:, pl.ds(pl.multiple_of(row * width, width), width)], ones], axis=0)
        dims = (((1,), (1,)), ((), ()))
        sums[col] += lax.dot_general(factor, high, dims, preferred_element_type=F32) + lax.dot_general(
            factor, low, dims, preferred_element_type=F32
        )
    each = LANES // sums.shape[2]
    across = blocks // each
    half = out_ref.shape[1] // 9
    for j in range(across):
        wide = jnp.concatenate([sums[c] for c in range(each * j, each * j + each)], axis=1)
        for g in range(count // 8):
            owner = g * across + j
            start = owner % half * 9
            out_ref[owner // half, start:start + 8] = wide[8 * g:8 * g + 8]
            out_ref[owner // half, start + 8:start + 9] = wide[count:count + 1]


def core_sums(parts_ref, out_ref):
    mine = my_core()
    value = parts_ref[0, mine] + parts_ref[1, mine]
    for i in range(out_ref.shape[0]):
        for r in range(9):
            out_ref[i, r] = value[9 * i + r:9 * i + r + 1]


def finish(parts_ref, out_ref):
    both = jnp.sum(parts_ref[...], axis=0)
    value = jnp.concatenate([both[r] for r in range(8)], axis=0)
    copies(out_ref, value / both[8])


def my_core():
    return lax.axis_index("core")


def spread(parts, axis):
    return lax.all_to_all(parts, axis, 0, 0)


def pair(parts):
    return lax.all_gather(parts, "core")


def call(kernel, out_shape, in_specs, scratch_shapes=(), limit=40 * MIB):
    single = not isinstance(out_shape, tuple)
    return pl.pallas_call(
        kernel,
        out_shape=out_shape,
        in_specs=in_specs,
        out_specs=vmem(1)[0] if single else tuple(vmem(len(out_shape))),
        scratch_shapes=list(scratch_shapes),
        compiler_params=pltpu.CompilerParams(vmem_limit_bytes=limit),
    )


def on_device(n_core, n_z, n_state, energies, tile_rows, tile_cols, start_free, temps, betas, counts, basis):
    slots, state_block, sample_block = energies.shape
    state_dev = start_free.shape[0]
    blocks = state_dev // state_block
    blocks_samp = basis.shape[1] // sample_block
    cut = sample_block // LANES
    rows = state_dev // LANES
    count = basis.shape[0]
    shape = lambda *dims: jax.ShapeDtypeStruct(dims, F32)
    by_state = (blocks + 1, state_block, LANES)
    place = [
        pltpu.SMEM(tile_rows.shape, jnp.int32), pltpu.SMEM(tile_cols.shape, jnp.int32), pltpu.SemaphoreType.DMA((3,))
    ]
    flat = pltpu.VMEM((rows, LANES), F32)
    whole = pltpu.VMEM((rows, LANES), jnp.int32)
    by_slot = pltpu.VMEM((cut * slots, LANES), F32)

    free, temps, counts = (vector.reshape(rows, LANES) for vector in (start_free, temps, counts))

    parts = call(
        first_samples,
        shape(n_state * (cut * slots + 1), LANES),
        hbm(7),
        place[:2] + [
            pltpu.SMEM(betas.shape, F32),
            pltpu.VMEM(energies.shape, F32),
            flat, whole, whole, pltpu.VMEM(by_state, F32), pltpu.VMEM(by_state, F32), by_slot, by_slot,
            pltpu.SemaphoreType.DMA((6 + slots // UNROLL,)),
        ],
        FIRST_VMEM,
    )(tile_rows, tile_cols, betas, energies, free, temps, counts)
    parts = spread(parts.reshape(n_state, cut * slots + 1, 1, LANES), "state").reshape(-1, LANES)
    parts, values, hot = call(
        first_states,
        (
            shape(rows, LANES), shape(*energies.shape),
            jax.ShapeDtypeStruct((blocks_samp, n_state * slots), BF16),
        ),
        vmem(6),
        [
            pltpu.VMEM(by_state, F32), pltpu.VMEM((cut * blocks_samp, LANES), F32),
            pltpu.VMEM(by_state, F32), pltpu.VMEM(by_state, F32),
        ],
    )(tile_rows.reshape(1, slots), tile_cols.reshape(1, slots), betas.reshape(1, -1), temps, energies, parts)
    parts = pair(parts)
    parts = call(both_cores, shape(n_z, rows, LANES), vmem(1))(parts)
    parts = spread(parts, "z")
    parts, weights = call(
        second_samples,
        (shape(n_state, cut * slots, LANES), shape(*energies.shape)),
        vmem(4),
        [pltpu.VMEM(by_state, F32), by_slot],
    )(tile_cols.reshape(1, slots), values, counts, parts)
    parts = spread(parts, "state")
    parts = call(
        second_states,
        shape(n_core, n_z * 9, LANES),
        vmem(6),
        [
            pltpu.VMEM((cut * blocks_samp, LANES), F32), pltpu.VMEM((blocks + 1, count + 16, state_block), F32)
        ],
    )(tile_rows.reshape(1, slots), tile_cols.reshape(1, slots), weights, hot, parts, basis)
    parts = pair(parts)
    parts = call(core_sums, shape(n_z, 9, 1, LANES), vmem(1))(parts)
    parts = spread(parts, "z")
    parts = call(finish, shape(n_z, 8, LANES), vmem(1))(parts)
    parts = spread(parts, "z")
    parts = pair(parts)
    return parts.reshape(count // 8, rows, 8, LANES).transpose(0, 2, 1, 3).reshape(count, state_dev)


def solution(mesh):
    n_samp, n_state = mesh.shape["samp"], mesh.shape["state"]
    n_core = 2
    n_z = n_samp // n_core
    cut = Mesh(mesh.devices.reshape(n_z, n_core, n_state), ("z", "core", "state"))
    samp = ("z", "core")

    def run(*args):
        return on_device(n_core, n_z, n_state, *args)

    return jax.shard_map(
        run,
        mesh=cut,
        in_specs=(
            P(("z", "core", "state"), None, None),
            P(("z", "core", "state")),
            P(("z", "core", "state")),
            P("state"),
            P("state"),
            P(),
            P("state"),
            P(None, samp),
        ),
        out_specs=P(None, "state"),
        check_vma=False,
    )
```

```python
import jax
import jax.numpy as jnp
from jax import lax
from jax.experimental import pallas as pl
from jax.experimental.pallas import tpu as pltpu
from jax.sharding import Mesh, PartitionSpec as P

NEG = -1e30
TINY = 1e-30
LANES = 128
MIB = 1024 * 1024
COST = 10**10
F32 = jnp.float32
BF16 = jnp.bfloat16
LOG2E = 1.4426950408889634
STEP = 96.0
BASE = -400.0
LAST = 11.0
BITS = 10.0


def vmem(count):
    return [pl.BlockSpec(memory_space=pltpu.VMEM)] * count


def state_beta(temps, betas_ref):
    beta = jnp.zeros(temps.shape, F32)
    for i in range(betas_ref.shape[-1]):
        beta = jnp.where(temps == i, betas_ref[:, i:i + 1], beta)
    return -LOG2E * beta


def log_count(counts_ref):
    return LOG2E * jnp.log(counts_ref[...].astype(F32))


def expand(rows, cols_ref, spare):
    turned = rows.T
    size = cols_ref.shape[1]
    each = LANES // size
    for j in range(rows.shape[0]):
        wide = jnp.broadcast_to(turned[:, j:j + 1], (LANES, LANES))
        for i in range(each):
            cols_ref[each * j + i] = wide[i * size:(i + 1) * size]
    cols_ref[cols_ref.shape[0] - 1] = jnp.full(cols_ref.shape[1:], spare, F32)


def halves(energies_ref, t):
    count = energies_ref.shape[2] // LANES
    return [energies_ref[t, :, h * LANES:(h + 1) * LANES] for h in range(count)]


def copies(out_ref, value):
    for i in range(out_ref.shape[0]):
        out_ref[i] = value


def log_sum(parts):
    top = jnp.max(parts, axis=0)
    return top + jnp.log2(jnp.sum(jnp.exp2(parts - top[None]), axis=0))


def row_sums(hot, values):
    total = None
    for _ in range(3):
        part = values.astype(BF16)
        values = values - part.astype(F32)
        product = jnp.dot(hot, part, preferred_element_type=F32)
        total = product if total is None else total + product
    return total


def by_half(parts_ref, half, slots):
    values = parts_ref[:, half * slots:(half + 1) * slots]
    return values.reshape(values.shape[0] * slots, LANES)


def begin(out_ref):
    out_ref[...] = jnp.zeros(out_ref.shape, F32)


def state_columns(betas_ref, free_ref, temps_ref, counts_ref, start_ref, beta_cols, bias_cols):
    expand(state_beta(temps_ref[...], betas_ref), beta_cols, 0.0)
    expand(log_count(counts_ref) + LOG2E * free_ref[...] + start_ref[...], bias_cols, NEG)


def first_samples(rows_ref, cols_ref, beta_cols, bias_cols, energies_ref, out_ref, slot, total):
    slots = energies_ref.shape[0]
    cut = energies_ref.shape[2] // LANES
    rows, cols = rows_ref[...], cols_ref[...]
    cols = [cols[0, t] for t in range(slots)]
    places = jnp.concatenate([rows.astype(F32), jnp.zeros((1, LANES - slots), F32)], axis=1)
    for t in range(slots):
        beta, bias = beta_cols[cols[t]], bias_cols[cols[t]]
        for h, energy in enumerate(halves(energies_ref, t)):
            score = bias + beta * energy
            peak = jnp.max(score, axis=0, keepdims=True)
            slot[h * slots + t:h * slots + t + 1] = peak
            total[h * slots + t:h * slots + t + 1] = jnp.sum(jnp.exp2(score - peak), axis=0, keepdims=True)
    whole = slot[...] + jnp.log2(jnp.maximum(total[...], 1.0))
    each = cut * slots + 1
    for i in range(out_ref.shape[0] // each):
        out_ref[i * each:(i + 1) * each - 1] = whole
        out_ref[(i + 1) * each - 1:(i + 1) * each] = places


def first_states(rows_ref, cols_ref, beta_cols, energies_ref, parts_ref, out_ref, values_ref, hot_ref,
                 drop, top, total):
    rows, cols = rows_ref[...], cols_ref[...]
    rows = [rows[0, t] for t in range(energies_ref.shape[0])]
    cols = [cols[0, t] for t in range(energies_ref.shape[0])]
    blocks = beta_cols.shape[0] - 1
    slots = energies_ref.shape[0]
    cut = energies_ref.shape[2] // LANES
    blocks_samp = drop.shape[0] // cut
    wide = []
    each = cut * slots + 1
    peers = parts_ref.shape[0] // each
    for j in range(peers * slots // LANES):
        places = jnp.zeros((1, LANES), F32)
        for i in range(LANES // slots):
            end = (j * (LANES // slots) + i + 1) * each
            place = parts_ref[end - 1:end]
            place = jnp.where(lax.broadcasted_iota(jnp.int32, place.shape, 1) < slots, place, 0.0)
            places = places + (pltpu.roll(place, i * slots, 1) if i else place)
        wide.append(places)
    wide = jnp.concatenate(wide, axis=1)
    row = lax.broadcasted_iota(jnp.int32, (blocks_samp, wide.shape[1]), 0).astype(F32)
    hot = jnp.where(row == wide, 1.0, 0.0).astype(BF16)
    hot_ref[...] = hot
    parts = jnp.concatenate(
        [
            jnp.concatenate(
                [parts_ref[i * each + h * slots:i * each + (h + 1) * slots] for i in range(peers)], axis=0
            )
            for h in range(cut)
        ],
        axis=1,
    )
    step = jnp.clip(jnp.floor((parts - BASE) * (1.0 / STEP)), 0.0, LAST)
    power = jnp.exp2(BITS * step).astype(BF16)
    found = jnp.maximum(jnp.dot(hot, power, preferred_element_type=F32), 1.0)
    step = jnp.floor(jnp.log2(found) * (1.0 / BITS) + 0.03)
    back = lax.dot_general(hot, step.astype(BF16), (((0,), (0,)), ((), ())), preferred_element_type=F32)
    whole = row_sums(hot, jnp.exp2(parts - (BASE + STEP * back)))
    whole = BASE + STEP * step + jnp.log2(jnp.maximum(whole, 0.5))
    for h in range(cut):
        drop[h * blocks_samp:(h + 1) * blocks_samp] = whole[:, h * LANES:(h + 1) * LANES]
    top[...] = jnp.full(top.shape, NEG, F32)
    total[...] = jnp.zeros(total.shape, F32)

    for t in range(slots):
        row, col = rows[t], cols[t]
        beta = beta_cols[col]
        most = top[col]
        for h, energy in enumerate(halves(energies_ref, t)):
            value = beta * energy - drop[pl.ds(h * blocks_samp + row, 1)]
            values_ref[t, :, h * LANES:(h + 1) * LANES] = value
            most = jnp.maximum(most, value)
        top[col] = most
    for t in range(slots):
        col = cols[t]
        most = top[col]
        part = total[col]
        for value in halves(values_ref, t):
            part = part + jnp.exp2(value - most)
        total[col] = part
    each = LANES // top.shape[1]
    for j in range(blocks // each):
        column = range(each * j, each * j + each)
        tops = jnp.concatenate([top[c] for c in column], axis=0).T
        sums = jnp.concatenate([total[c] for c in column], axis=0).T
        peak = jnp.max(tops, axis=0, keepdims=True)
        whole = jnp.sum(sums * jnp.exp2(tops - peak), axis=0, keepdims=True)
        out_ref[j:j + 1] = peak + jnp.log2(jnp.maximum(whole, 1.0))


def both_cores(parts_ref, out_ref):
    copies(out_ref, log_sum(parts_ref[...]))


def second_samples(cols_ref, values_ref, counts_ref, parts_ref, out_ref, weights_ref,
                   bias_cols, slot):
    cols = cols_ref[...]
    cols = [cols[0, t] for t in range(values_ref.shape[0])]
    slots = values_ref.shape[0]
    expand(log_count(counts_ref) - log_sum(parts_ref[...]), bias_cols, NEG)
    for t in range(slots):
        bias = bias_cols[cols[t]]
        for h, value in enumerate(halves(values_ref, t)):
            part = jnp.exp2(bias + value)
            weights_ref[t, :, h * LANES:(h + 1) * LANES] = part
            slot[h * slots + t:h * slots + t + 1] = jnp.maximum(
                jnp.sum(part, axis=0, keepdims=True), jnp.max(part, axis=0, keepdims=True)
            )
    copies(out_ref, slot[...])


def second_states(rows_ref, cols_ref, weights_ref, hot_ref, parts_ref, basis_ref, out_ref, scale, sums):
    rows, cols = rows_ref[...], cols_ref[...]
    rows = [rows[0, t] for t in range(weights_ref.shape[0])]
    cols = [cols[0, t] for t in range(weights_ref.shape[0])]
    blocks = sums.shape[0] - 1
    slots = weights_ref.shape[0]
    count = basis_ref.shape[0]
    width = weights_ref.shape[2]
    cut = width // LANES
    blocks_samp = scale.shape[0] // cut
    parts = jnp.concatenate([by_half(parts_ref, h, slots) for h in range(cut)], axis=1)
    whole = 1.0 / jnp.maximum(row_sums(hot_ref[...], parts), TINY)
    for h in range(cut):
        scale[h * blocks_samp:(h + 1) * blocks_samp] = whole[:, h * LANES:(h + 1) * LANES]
    sums[...] = jnp.zeros(sums.shape, F32)
    ones = jnp.ones((sums.shape[1] - count, width), BF16)
    for t in range(slots):
        row, col = rows[t], cols[t]
        weight = jnp.concatenate(
            [part * scale[pl.ds(h * blocks_samp + row, 1)] for h, part in enumerate(halves(weights_ref, t))], axis=1
        )
        high = weight.astype(BF16)
        low = (weight - high.astype(F32)).astype(BF16)
        factor = jnp.concatenate([basis_ref[:, pl.ds(pl.multiple_of(row * width, width), width)], ones], axis=0)
        dims = (((1,), (1,)), ((), ()))
        sums[col] += lax.dot_general(factor, high, dims, preferred_element_type=F32) + lax.dot_general(
            factor, low, dims, preferred_element_type=F32
        )
    each = LANES // sums.shape[2]
    across = blocks // each
    half = out_ref.shape[1] // 9
    for j in range(across):
        wide = jnp.concatenate([sums[c] for c in range(each * j, each * j + each)], axis=1)
        for g in range(count // 8):
            owner = g * across + j
            start = owner % half * 9
            out_ref[owner // half, start:start + 8] = wide[8 * g:8 * g + 8]
            out_ref[owner // half, start + 8:start + 9] = wide[count:count + 1]


def core_sums(parts_ref, out_ref):
    mine = my_core()
    value = parts_ref[0, mine] + parts_ref[1, mine]
    for i in range(out_ref.shape[0]):
        for r in range(9):
            out_ref[i, r] = value[9 * i + r:9 * i + r + 1]


def finish(parts_ref, out_ref):
    both = jnp.sum(parts_ref[...], axis=0)
    value = jnp.concatenate([both[r] for r in range(8)], axis=0)
    copies(out_ref, value / both[8])


def my_core():
    return lax.axis_index("core")


def spread(parts, axis):
    return lax.all_to_all(parts, axis, 0, 0)


def pair(parts):
    return lax.all_gather(parts, "core")


def call(kernel, out_shape, in_specs, scratch_shapes=(), cost=None):
    single = not isinstance(out_shape, tuple)
    return pl.pallas_call(
        kernel,
        out_shape=out_shape,
        in_specs=in_specs,
        out_specs=vmem(1)[0] if single else tuple(vmem(len(out_shape))),
        scratch_shapes=list(scratch_shapes),
        compiler_params=pltpu.CompilerParams(vmem_limit_bytes=40 * MIB),
        cost_estimate=cost,
    )


def on_device(n_core, n_z, n_state, energies, tile_rows, tile_cols, start_free, temps, betas, counts, basis):
    slots, state_block, sample_block = energies.shape
    state_dev = start_free.shape[0]
    blocks = state_dev // state_block
    blocks_samp = basis.shape[1] // sample_block
    cut = sample_block // LANES
    rows = state_dev // LANES
    count = basis.shape[0]
    shape = lambda *dims: jax.ShapeDtypeStruct(dims, F32)
    by_state = (blocks + 1, state_block, LANES)
    by_slot = pltpu.VMEM((cut * slots, LANES), F32)
    free, temps, counts = (vector.reshape(rows, LANES) for vector in (start_free, temps, counts))

    tile_rows, tile_cols, betas = (vector.reshape(1, -1) for vector in (tile_rows, tile_cols, betas))
    start = call(begin, shape(rows, LANES), [], cost=pl.CostEstimate(flops=COST, bytes_accessed=0, transcendentals=0))()
    beta, bias = call(state_columns, (shape(*by_state), shape(*by_state)), vmem(5))(betas, free, temps, counts, start)
    parts = call(first_samples, shape(n_state * (cut * slots + 1), LANES), vmem(5), [by_slot, by_slot])(
        tile_rows, tile_cols, beta, bias, energies
    )
    parts = spread(parts.reshape(n_state, cut * slots + 1, 1, LANES), "state").reshape(-1, LANES)
    parts, values, hot = call(
        first_states,
        (
            shape(rows, LANES), shape(*energies.shape),
            jax.ShapeDtypeStruct((blocks_samp, n_state * slots), BF16),
        ),
        vmem(5),
        [
            pltpu.VMEM((cut * blocks_samp, LANES), F32),
            pltpu.VMEM(by_state, F32), pltpu.VMEM(by_state, F32),
        ],
    )(tile_rows, tile_cols, beta, energies, parts)
    parts = pair(parts)
    parts = call(both_cores, shape(n_z, rows, LANES), vmem(1))(parts)
    parts = spread(parts, "z")
    parts, weights = call(
        second_samples,
        (shape(n_state, cut * slots, LANES), shape(*energies.shape)),
        vmem(4),
        [pltpu.VMEM(by_state, F32), by_slot],
    )(tile_cols, values, counts, parts)
    parts = spread(parts, "state")
    parts = call(
        second_states,
        shape(n_core, n_z * 9, LANES),
        vmem(6),
        [
            pltpu.VMEM((cut * blocks_samp, LANES), F32), pltpu.VMEM((blocks + 1, count + 16, state_block), F32)
        ],
    )(tile_rows, tile_cols, weights, hot, parts, basis)
    parts = pair(parts)
    parts = call(core_sums, shape(n_z, 9, 1, LANES), vmem(1))(parts)
    parts = spread(parts, "z")
    parts = call(finish, shape(n_z, 8, LANES), vmem(1))(parts)
    parts = spread(parts, "z")
    parts = pair(parts)
    return parts.reshape(count // 8, rows, 8, LANES).transpose(0, 2, 1, 3).reshape(count, state_dev)


def solution(mesh):
    n_samp, n_state = mesh.shape["samp"], mesh.shape["state"]
    n_core = 2
    n_z = n_samp // n_core
    cut = Mesh(mesh.devices.reshape(n_z, n_core, n_state), ("z", "core", "state"))
    samp = ("z", "core")

    def run(*args):
        return on_device(n_core, n_z, n_state, *args)

    return jax.shard_map(
        run,
        mesh=cut,
        in_specs=(
            P(("z", "core", "state"), None, None),
            P(("z", "core", "state")),
            P(("z", "core", "state")),
            P("state"),
            P("state"),
            P(),
            P("state"),
            P(None, samp),
        ),
        out_specs=P(None, "state"),
        check_vma=False,
    )
```

```python
import jax
import jax.numpy as jnp
from jax import lax
from jax.experimental import pallas as pl
from jax.experimental.pallas import tpu as pltpu
from jax.sharding import Mesh, PartitionSpec as P

NEG = -1e30
TINY = 1e-30
LANES = 128
MIB = 1024 * 1024
COST = 10**10
F32 = jnp.float32
BF16 = jnp.bfloat16
LOG2E = 1.4426950408889634
STEP = 96.0
BASE = -400.0
LAST = 11.0
BITS = 10.0


def vmem(count):
    return [pl.BlockSpec(memory_space=pltpu.VMEM)] * count


def state_beta(temps, betas_ref):
    beta = jnp.zeros(temps.shape, F32)
    for i in range(betas_ref.shape[-1]):
        beta = jnp.where(temps == i, betas_ref[:, i:i + 1], beta)
    return -LOG2E * beta


def log_count(counts_ref):
    return LOG2E * jnp.log(counts_ref[...].astype(F32))


def expand(rows, cols_ref, spare):
    turned = rows.T
    size = cols_ref.shape[1]
    each = LANES // size
    for j in range(rows.shape[0]):
        wide = jnp.broadcast_to(turned[:, j:j + 1], (LANES, LANES))
        for i in range(each):
            cols_ref[each * j + i] = wide[i * size:(i + 1) * size]
    cols_ref[cols_ref.shape[0] - 1] = jnp.full(cols_ref.shape[1:], spare, F32)


def halves(energies_ref, t):
    count = energies_ref.shape[2] // LANES
    return [energies_ref[t, :, h * LANES:(h + 1) * LANES] for h in range(count)]


def copies(out_ref, value):
    for i in range(out_ref.shape[0]):
        out_ref[i] = value


def log_sum(parts):
    top = jnp.max(parts, axis=0)
    return top + jnp.log2(jnp.sum(jnp.exp2(parts - top[None]), axis=0))


def row_sums(hot, values):
    total = None
    for _ in range(2):
        part = values.astype(BF16)
        values = values - part.astype(F32)
        product = jnp.dot(hot, part, preferred_element_type=F32)
        total = product if total is None else total + product
    return total


def by_half(parts_ref, half, slots):
    values = parts_ref[:, half * slots:(half + 1) * slots]
    return values.reshape(values.shape[0] * slots, LANES)


def begin(out_ref):
    out_ref[...] = jnp.zeros(out_ref.shape, F32)


def state_columns(betas_ref, free_ref, temps_ref, counts_ref, start_ref, beta_cols, bias_cols, logs_ref):
    expand(state_beta(temps_ref[...], betas_ref), beta_cols, 0.0)
    logs_ref[...] = log_count(counts_ref)
    expand(logs_ref[...] + LOG2E * free_ref[...] + start_ref[...], bias_cols, NEG)


def first_samples(rows_ref, cols_ref, beta_cols, bias_cols, energies_ref, out_ref, slot, total):
    slots = energies_ref.shape[0]
    cut = energies_ref.shape[2] // LANES
    rows, cols = rows_ref[...], cols_ref[...]
    cols = [cols[0, t] for t in range(slots)]
    places = jnp.concatenate([rows.astype(F32), jnp.zeros((1, LANES - slots), F32)], axis=1)
    for t in range(slots):
        beta, bias = beta_cols[cols[t]], bias_cols[cols[t]]
        for h, energy in enumerate(halves(energies_ref, t)):
            score = bias + beta * energy
            peak = jnp.max(score, axis=0, keepdims=True)
            slot[h * slots + t:h * slots + t + 1] = peak
            total[h * slots + t:h * slots + t + 1] = jnp.sum(jnp.exp2(score - peak), axis=0, keepdims=True)
    whole = slot[...] + jnp.log2(jnp.maximum(total[...], 1.0))
    each = cut * slots + 1
    for i in range(out_ref.shape[0] // each):
        out_ref[i * each:(i + 1) * each - 1] = whole
        out_ref[(i + 1) * each - 1:(i + 1) * each] = places


def first_states(rows_ref, cols_ref, beta_cols, energies_ref, parts_ref, out_ref, values_ref, hot_ref,
                 drop, top, total):
    rows, cols = rows_ref[...], cols_ref[...]
    rows = [rows[0, t] for t in range(energies_ref.shape[0])]
    cols = [cols[0, t] for t in range(energies_ref.shape[0])]
    blocks = beta_cols.shape[0] - 1
    slots = energies_ref.shape[0]
    cut = energies_ref.shape[2] // LANES
    blocks_samp = drop.shape[0] // cut
    wide = []
    each = cut * slots + 1
    peers = parts_ref.shape[0] // each
    for j in range(peers * slots // LANES):
        places = jnp.zeros((1, LANES), F32)
        for i in range(LANES // slots):
            end = (j * (LANES // slots) + i + 1) * each
            place = parts_ref[end - 1:end]
            place = jnp.where(lax.broadcasted_iota(jnp.int32, place.shape, 1) < slots, place, 0.0)
            places = places + (pltpu.roll(place, i * slots, 1) if i else place)
        wide.append(places)
    wide = jnp.concatenate(wide, axis=1)
    row = lax.broadcasted_iota(jnp.int32, (blocks_samp, wide.shape[1]), 0).astype(F32)
    hot = jnp.where(row == wide, 1.0, 0.0).astype(BF16)
    hot_ref[...] = hot
    parts = jnp.concatenate(
        [
            jnp.concatenate(
                [parts_ref[i * each + h * slots:i * each + (h + 1) * slots] for i in range(peers)], axis=0
            )
            for h in range(cut)
        ],
        axis=1,
    )
    step = jnp.clip(jnp.floor((parts - BASE) * (1.0 / STEP)), 0.0, LAST)
    power = jnp.exp2(BITS * step).astype(BF16)
    found = jnp.maximum(jnp.dot(hot, power, preferred_element_type=F32), 1.0)
    step = jnp.floor(jnp.log2(found) * (1.0 / BITS) + 0.03)
    back = lax.dot_general(hot, step.astype(BF16), (((0,), (0,)), ((), ())), preferred_element_type=F32)
    whole = row_sums(hot, jnp.exp2(parts - (BASE + STEP * back)))
    whole = BASE + STEP * step + jnp.log2(jnp.maximum(whole, 0.5))
    for h in range(cut):
        drop[h * blocks_samp:(h + 1) * blocks_samp] = whole[:, h * LANES:(h + 1) * LANES]
    top[...] = jnp.full(top.shape, NEG, F32)
    total[...] = jnp.zeros(total.shape, F32)

    for t in range(slots):
        row, col = rows[t], cols[t]
        beta = beta_cols[col]
        most = top[col]
        for h, energy in enumerate(halves(energies_ref, t)):
            value = beta * energy - drop[pl.ds(h * blocks_samp + row, 1)]
            values_ref[t, :, h * LANES:(h + 1) * LANES] = value
            most = jnp.maximum(most, value)
        top[col] = most
    for t in range(slots):
        col = cols[t]
        most = top[col]
        part = total[col]
        for value in halves(values_ref, t):
            part = part + jnp.exp2(value - most)
        total[col] = part
    each = LANES // top.shape[1]
    for j in range(blocks // each):
        column = range(each * j, each * j + each)
        tops = jnp.concatenate([top[c] for c in column], axis=0).T
        sums = jnp.concatenate([total[c] for c in column], axis=0).T
        peak = jnp.max(tops, axis=0, keepdims=True)
        whole = jnp.sum(sums * jnp.exp2(tops - peak), axis=0, keepdims=True)
        out_ref[j:j + 1] = peak + jnp.log2(jnp.maximum(whole, 1.0))


def both_cores(parts_ref, out_ref):
    copies(out_ref, log_sum(parts_ref[...]))


def second_samples(cols_ref, values_ref, logs_ref, parts_ref, out_ref, weights_ref,
                   bias_cols, slot):
    cols = cols_ref[...]
    cols = [cols[0, t] for t in range(values_ref.shape[0])]
    slots = values_ref.shape[0]
    expand(logs_ref[...] - log_sum(parts_ref[...]), bias_cols, NEG)
    for t in range(slots):
        bias = bias_cols[cols[t]]
        for h, value in enumerate(halves(values_ref, t)):
            part = jnp.exp2(bias + value)
            weights_ref[t, :, h * LANES:(h + 1) * LANES] = part
            slot[h * slots + t:h * slots + t + 1] = jnp.maximum(
                jnp.sum(part, axis=0, keepdims=True), jnp.max(part, axis=0, keepdims=True)
            )
    copies(out_ref, slot[...])


def second_states(rows_ref, cols_ref, weights_ref, hot_ref, parts_ref, basis_ref, out_ref, scale, sums):
    rows, cols = rows_ref[...], cols_ref[...]
    rows = [rows[0, t] for t in range(weights_ref.shape[0])]
    cols = [cols[0, t] for t in range(weights_ref.shape[0])]
    blocks = sums.shape[0] - 1
    slots = weights_ref.shape[0]
    count = basis_ref.shape[0]
    width = weights_ref.shape[2]
    cut = width // LANES
    blocks_samp = scale.shape[0] // cut
    parts = jnp.concatenate([by_half(parts_ref, h, slots) for h in range(cut)], axis=1)
    whole = 1.0 / jnp.maximum(row_sums(hot_ref[...], parts), TINY)
    for h in range(cut):
        scale[h * blocks_samp:(h + 1) * blocks_samp] = whole[:, h * LANES:(h + 1) * LANES]
    sums[...] = jnp.zeros(sums.shape, F32)
    ones = jnp.ones((sums.shape[1] - count, width), BF16)
    for t in range(slots):
        row, col = rows[t], cols[t]
        weight = jnp.concatenate(
            [part * scale[pl.ds(h * blocks_samp + row, 1)] for h, part in enumerate(halves(weights_ref, t))], axis=1
        )
        high = weight.astype(BF16)
        low = (weight - high.astype(F32)).astype(BF16)
        factor = jnp.concatenate([basis_ref[:, pl.ds(pl.multiple_of(row * width, width), width)], ones], axis=0)
        dims = (((1,), (1,)), ((), ()))
        sums[col] += lax.dot_general(factor, high, dims, preferred_element_type=F32) + lax.dot_general(
            factor, low, dims, preferred_element_type=F32
        )
    each = LANES // sums.shape[2]
    across = blocks // each
    half = out_ref.shape[1] // 9
    for j in range(across):
        wide = jnp.concatenate([sums[c] for c in range(each * j, each * j + each)], axis=1)
        for g in range(count // 8):
            owner = g * across + j
            start = owner % half * 9
            out_ref[owner // half, start:start + 8] = wide[8 * g:8 * g + 8]
            out_ref[owner // half, start + 8:start + 9] = wide[count:count + 1]


def core_sums(parts_ref, out_ref):
    mine = my_core()
    value = parts_ref[0, mine] + parts_ref[1, mine]
    for i in range(out_ref.shape[0]):
        for r in range(9):
            out_ref[i, r] = value[9 * i + r:9 * i + r + 1]


def finish(parts_ref, out_ref):
    both = jnp.sum(parts_ref[...], axis=0)
    value = jnp.concatenate([both[r] for r in range(8)], axis=0)
    copies(out_ref, value / both[8])


def my_core():
    return lax.axis_index("core")


def spread(parts, axis):
    return lax.all_to_all(parts, axis, 0, 0)


def pair(parts):
    return lax.all_gather(parts, "core")


def call(kernel, out_shape, in_specs, scratch_shapes=(), cost=None):
    single = not isinstance(out_shape, tuple)
    return pl.pallas_call(
        kernel,
        out_shape=out_shape,
        in_specs=in_specs,
        out_specs=vmem(1)[0] if single else tuple(vmem(len(out_shape))),
        scratch_shapes=list(scratch_shapes),
        compiler_params=pltpu.CompilerParams(vmem_limit_bytes=40 * MIB),
        cost_estimate=cost,
    )


def on_device(n_core, n_z, n_state, energies, tile_rows, tile_cols, start_free, temps, betas, counts, basis):
    slots, state_block, sample_block = energies.shape
    state_dev = start_free.shape[0]
    blocks = state_dev // state_block
    blocks_samp = basis.shape[1] // sample_block
    cut = sample_block // LANES
    rows = state_dev // LANES
    count = basis.shape[0]
    shape = lambda *dims: jax.ShapeDtypeStruct(dims, F32)
    by_state = (blocks + 1, state_block, LANES)
    by_slot = pltpu.VMEM((cut * slots, LANES), F32)
    free, temps, counts = (vector.reshape(rows, LANES) for vector in (start_free, temps, counts))

    tile_rows, tile_cols, betas = (vector.reshape(1, -1) for vector in (tile_rows, tile_cols, betas))
    start = call(begin, shape(rows, LANES), [], cost=pl.CostEstimate(flops=COST, bytes_accessed=0, transcendentals=0))()
    beta, bias, logs = call(state_columns, (shape(*by_state), shape(*by_state), shape(rows, LANES)), vmem(5))(
        betas, free, temps, counts, start
    )
    parts = call(first_samples, shape(n_state * (cut * slots + 1), LANES), vmem(5), [by_slot, by_slot])(
        tile_rows, tile_cols, beta, bias, energies
    )
    parts = spread(parts.reshape(n_state, cut * slots + 1, 1, LANES), "state").reshape(-1, LANES)
    parts, values, hot = call(
        first_states,
        (
            shape(rows, LANES), shape(*energies.shape),
            jax.ShapeDtypeStruct((blocks_samp, n_state * slots), BF16),
        ),
        vmem(5),
        [
            pltpu.VMEM((cut * blocks_samp, LANES), F32),
            pltpu.VMEM(by_state, F32), pltpu.VMEM(by_state, F32),
        ],
    )(tile_rows, tile_cols, beta, energies, parts)
    parts = pair(parts)
    parts = call(both_cores, shape(n_z, rows, LANES), vmem(1))(parts)
    parts = spread(parts, "z")
    parts, weights = call(
        second_samples,
        (shape(n_state, cut * slots, LANES), shape(*energies.shape)),
        vmem(4),
        [pltpu.VMEM(by_state, F32), by_slot],
    )(tile_cols, values, logs, parts)
    parts = spread(parts, "state")
    parts = call(
        second_states,
        shape(n_core, n_z * 9, LANES),
        vmem(6),
        [
            pltpu.VMEM((cut * blocks_samp, LANES), F32), pltpu.VMEM((blocks + 1, count + 16, state_block), F32)
        ],
    )(tile_rows, tile_cols, weights, hot, parts, basis)
    parts = pair(parts)
    parts = call(core_sums, shape(n_z, 9, 1, LANES), vmem(1))(parts)
    parts = spread(parts, "z")
    parts = call(finish, shape(n_z, 8, LANES), vmem(1))(parts)
    parts = spread(parts, "z")
    parts = pair(parts)
    return parts.reshape(count // 8, rows, 8, LANES).transpose(0, 2, 1, 3).reshape(count, state_dev)


def solution(mesh):
    n_samp, n_state = mesh.shape["samp"], mesh.shape["state"]
    n_core = 2
    n_z = n_samp // n_core
    cut = Mesh(mesh.devices.reshape(n_z, n_core, n_state), ("z", "core", "state"))
    samp = ("z", "core")

    def run(*args):
        return on_device(n_core, n_z, n_state, *args)

    return jax.shard_map(
        run,
        mesh=cut,
        in_specs=(
            P(("z", "core", "state"), None, None),
            P(("z", "core", "state")),
            P(("z", "core", "state")),
            P("state"),
            P("state"),
            P(),
            P("state"),
            P(None, samp),
        ),
        out_specs=P(None, "state"),
        check_vma=False,
    )
```
